512 devices in a mesh: fsdp: 64 (over x, z, core), tensor: 8 (over y).
Axes of the slice: x: 4, y: 8, z: 8, core: 2. Of those that a mesh axis runs over, the one named last changes fastest.
Arguments:
- momentum: float32 [8192, 28672], P('fsdp', 'tensor')
- gradient: bfloat16 [8192, 28672], P('fsdp', 'tensor'), may hold values from -6 to 6
- right_factor: float32 [28672, 256], P(('tensor', 'fsdp')), may hold values from -6 to 6
Outputs:
- new_momentum: float32 [8192, 28672], P('fsdp', 'tensor')
- new_right: float32 [28672, 256], P(('tensor', 'fsdp'))
- row_factor: float32 [8192, 256], P('fsdp')
The draws below stay inside these ranges and needn't reach their ends.
All inputs are finite; a program needn't handle non-finite values.
Results may differ from the reference program's by a relative error of at most 0.0003.
Values sent between devices are 32-bit elements; how exact they have to be, the bound alone decides.
No kernel may reach another device: no remote copies, remote signals or barrier semaphores. Data moves between devices by JAX's collectives and lax.ppermute only.
A program may use at most 64 MiB of HBM per device.

```python
import math
import jax
import jax.numpy as jnp
from jax import lax

ROWS = 8192
COLS = 28672
RANK = 256


def draw_momentum(key, part):
    key = jax.random.fold_in(key, 7)
    key_values, key_rows, key_cols = jax.random.split(key, 3)
    ramp_rows = jnp.arange(ROWS, dtype=jnp.float32) / ROWS
    ramp_cols = jnp.arange(COLS, dtype=jnp.float32) / COLS
    values = jax.random.normal(key_values, (ROWS, COLS), jnp.float32)
    spread = math.log(10.0 / 3.0)
    row_scale = jnp.exp(math.log(3.0) * ramp_rows + spread * jax.random.uniform(key_rows, (ROWS,), jnp.float32))
    col_scale = jnp.exp(math.log(3.0) * ramp_cols + spread * jax.random.uniform(key_cols, (COLS,), jnp.float32))
    return values * row_scale[:, None] * col_scale[None, :]


def level_of(stream_key, shape, shards, smallest, largest):
    gain, own = 1.0, jax.random.fold_in(stream_key, 6)
    for axis_at, blocks in shards:
        steps = jnp.exp(jax.random.uniform(jax.random.fold_in(own, axis_at), (blocks,), jnp.float32, smallest / len(shards), largest / len(shards)))
        gain = gain * jnp.repeat(steps, shape[axis_at] // blocks).reshape([-1 if axis == axis_at else 1 for axis in range(len(shape))])
    return gain


def centred(rng, dims, deviation, most, cuts=(), kind=jnp.bfloat16):
    loudness = level_of(rng, dims, cuts, -0.22, 0.18) if cuts else 1.0
    values = jax.random.normal(rng, dims, jnp.float32) * deviation * loudness
    return jnp.minimum(jnp.maximum(values, -most), most).astype(kind)


def setup_inputs(seed: int = 0) -> dict:
    key_list = jax.random.split(jax.random.key(seed), 4)
    return {
        "momentum": draw_momentum(jax.random.fold_in(key_list[3], 71), 0),
        "gradient": centred(key_list[1], (ROWS, COLS), 1.0, 6.0, ((0, 64), (1, 8))),
        "right_factor": centred(key_list[2], (COLS, RANK), 1.0, 6.0, ((0, 512),), jnp.float32),
    }


highest = lax.Precision.HIGHEST

def reference(momentum, gradient, right_factor):
    buffer = momentum + gradient.astype(jnp.float32)
    power_rows = jnp.dot(buffer.astype(jnp.float32), right_factor.astype(jnp.float32), precision=highest, preferred_element_type=jnp.float32)
    gram_matrix = jnp.dot(power_rows.T.astype(jnp.float32), power_rows.astype(jnp.float32), precision=highest, preferred_element_type=jnp.float32)
    lower_factor = jnp.linalg.cholesky(gram_matrix)
    orthonormal = jax.scipy.linalg.solve_triangular(lower_factor, power_rows.T, lower=True).T
    column_factor = jnp.dot(buffer.T.astype(jnp.float32), orthonormal.astype(jnp.float32), precision=highest, preferred_element_type=jnp.float32)
    new_momentum = buffer - 0.05 * jnp.dot(orthonormal.astype(jnp.float32), column_factor.T.astype(jnp.float32), precision=highest, preferred_element_type=jnp.float32)
    col_scale = jnp.sqrt(lax.optimization_barrier(jnp.mean(column_factor * column_factor, axis=0)) + 1e-06)
    new_right = column_factor / col_scale
    row_factor = orthonormal * math.sqrt(ROWS)
    return (new_momentum, new_right, row_factor)
```

```python
import math

import jax
import jax.numpy as jnp
import numpy as np
from jax import lax
from jax.experimental import pallas as pl
from jax.experimental.pallas import tpu as pltpu
from jax.sharding import Mesh, PartitionSpec as P

ROWS = 8192
COLS = 28672
RANK = 256
NX, NZ, NC, NY = 4, 8, 2, 8
CHIPS = NX * NZ
MY_ROWS = 128
MY_COLS = 3584
SHARD = 56
STEPS = 4
SOME = CHIPS // STEPS
CHUNK = SOME * NC * SHARD
BLOCK = 32
MACS = MY_ROWS * MY_COLS * RANK

highest = lax.Precision.HIGHEST
f32 = jnp.float32
bf16 = jnp.bfloat16
VMEM = pl.BlockSpec(memory_space=pltpu.VMEM)
SMEM = pl.BlockSpec(memory_space=pltpu.SMEM)
ANY = pl.BlockSpec(memory_space=pl.ANY)
HBM = pl.BlockSpec(memory_space=pltpu.HBM)


def dot(a, b, ca, cb, precision=highest):
    return lax.dot_general(
        a, b, (((ca,), (cb,)), ((), ())), precision=precision, preferred_element_type=f32
    )


def shape(*dims):
    return jax.ShapeDtypeStruct(dims, f32)


def in_hbm(*dims):
    return pltpu.HBM(dims, f32)


TOKEN = shape(8, 128)


def call(kernel, out_shape, in_specs, scratch=(), out_specs=None, flops=1_000_000, nbytes=100_000, limit=12):
    return pl.pallas_call(
        kernel,
        out_shape=out_shape,
        in_specs=in_specs,
        out_specs=out_specs or jax.tree.map(lambda _: VMEM, out_shape),
        scratch_shapes=scratch,
        compiler_params=pltpu.CompilerParams(vmem_limit_bytes=limit * 2**20),
        cost_estimate=pl.CostEstimate(
            flops=flops, bytes_accessed=nbytes, transcendentals=0
        ),
    )


def buffer_copies(mom, grad, mom_here, grad_here, sems, j):
    cols = pl.ds(j * CHUNK, CHUNK)
    return [
        pltpu.make_async_copy(mom.at[:, cols], mom_here.at[:, cols], sems.at[j, 0]),
        pltpu.make_async_copy(grad.at[:, cols], grad_here.at[:, cols], sems.at[j, 1]),
    ]


def factor_copies(core, own, other, full, sems, j):
    chips = pl.ds(j * SOME, SOME)
    return [
        pltpu.make_async_copy(own.at[chips], full.at[chips, core], sems.at[j, 2]),
        pltpu.make_async_copy(other.at[chips], full.at[chips, 1 - core], sems.at[j, 3]),
    ]


def buffer_chunk(mom, grad, j):
    cols = pl.ds(j * CHUNK, CHUNK)
    return mom[:, cols] + grad[:, cols].astype(f32)


BUFFER_SCRATCH = [pltpu.VMEM((MY_ROWS, MY_COLS), f32), pltpu.VMEM((MY_ROWS, MY_COLS), bf16)]
SEMS = [pltpu.SemaphoreType.DMA((STEPS, 4))]
FULL = [pltpu.VMEM((CHIPS, NC, SHARD, RANK), f32)]


def power_kernel(where, own, other, mom, grad, out, mom_here, grad_here, full, sems):
    copies = []
    for j in range(STEPS):
        copies.append(
            factor_copies(where[0], own, other, full, sems, j)
            + buffer_copies(mom, grad, mom_here, grad_here, sems, j)
        )
        for copy in copies[j]:
            copy.start()
    total = None
    for j in range(STEPS):
        for copy in copies[j]:
            copy.wait()
        part = full[pl.ds(j * SOME, SOME)].reshape(CHUNK, RANK)
        part = dot(buffer_chunk(mom_here, grad_here, j), part, 1, 0)
        total = part if total is None else total + part
    out[...] = total


def sum_spread_kernel(pieces, out):
    total = jnp.sum(pieces[...], axis=0)
    for i in range(out.shape[0]):
        out[i] = total


def gram_kernel(power, out, token):
    token[...] = jnp.zeros_like(token)
    gram = dot(power[...], power[...], 0, 0)
    for i in range(RANK // 8):
        for h in range(RANK // 128):
            out[i * 2 + h] = gram[i * 8 : i * 8 + 8, h * 128 : h * 128 + 128]


def column_kernel(where, power, mom, grad, after, keep, send, mom_here, grad_here, sems, kept, sent):
    copies = []
    for j in range(STEPS):
        copies.append(buffer_copies(mom, grad, mom_here, grad_here, sems, j))
        for copy in copies[j]:
            copy.start()
    for j in range(STEPS):
        for copy in copies[j]:
            copy.wait()
        part = dot(buffer_chunk(mom_here, grad_here, j), power[...], 0, 0)
        part = part.reshape(SOME, NC, SHARD, RANK)
        first = where[0] == 0
        chips = pl.ds(j * SOME, SOME)
        kept[chips] = jnp.where(first, part[:, 0], part[:, 1])
        sent[chips] = jnp.where(first, part[:, 1], part[:, 0])
        copies[j] = [
            pltpu.make_async_copy(sent.at[chips], send.at[chips], sems.at[j, 2]),
            pltpu.make_async_copy(kept.at[chips], keep.at[chips], sems.at[j, 3]),
        ]
        for copy in copies[j]:
            copy.start()
    for j in range(STEPS):
        for copy in copies[j]:
            copy.wait()


def add_kernel(mine, arrived, after, out, token):
    token[...] = jnp.zeros_like(token)
    out[...] = mine[...] + arrived[...]


def sum_kernel(pieces, after, out, token):
    token[...] = jnp.zeros_like(token)
    out[...] = jnp.sum(pieces[...], axis=0)


def copies_kernel(value, after, out):
    for i in range(out.shape[0]):
        out[i] = value[...]


def column_mine_kernel(pieces, after, mine, copies):
    total = jnp.sum(pieces[...], axis=0)
    mine[...] = total
    for i in range(NZ):
        copies[i] = total


def eliminate(a, blocks):
    row = lax.broadcasted_iota(jnp.int32, (BLOCK, BLOCK), 0)
    col = lax.broadcasted_iota(jnp.int32, (BLOCK, BLOCK), 1)
    eye = (row == col).astype(f32)
    wide = lax.broadcasted_iota(jnp.int32, (BLOCK, RANK), 1)
    for k in blocks:
        lo, hi = k * BLOCK, (k + 1) * BLOCK
        d = a[lo:hi, lo:hi]
        for j in range(BLOCK - 1):
            column = jnp.broadcast_to(d[:, j : j + 1], (BLOCK, BLOCK))
            pivot = jnp.broadcast_to(1.0 / column[j : j + 1, :], (BLOCK, BLOCK))
            line = jnp.broadcast_to(d[j : j + 1, :], (BLOCK, BLOCK))
            line = jnp.where(col == j, 1.0, line)
            rest = jnp.where(col == j, 0.0, d)
            d = jnp.where(row > j, rest - column * (line * pivot), d)
        diagonal = jnp.sum(d * eye, axis=1, keepdims=True)
        inner = (jnp.where(row > col, d, 0.0) + eye) * lax.rsqrt(diagonal)
        panel = a[lo:hi, :]
        panel = jnp.where((wide >= lo) & (wide < hi), 0.0, panel)
        panel = dot(inner, panel, 1, 0)
        a[lo:hi, :] = panel
        a[lo:hi, lo:hi] = inner
        panel = a[lo:hi, :]
        if hi < RANK:
            change = dot(panel, panel, 0, 0)
            a[hi:, lo:hi] = jnp.zeros((RANK - hi, BLOCK), f32)
            a[hi:, :] = a[hi:, :] - change[hi:, :]


def first_half_kernel(gram, after, a):
    for i in range(RANK // 8):
        for h in range(RANK // 128):
            a[i * 8 : i * 8 + 8, h * 128 : h * 128 + 128] = gram[i * 2 + h]
    eliminate(a, range(0, RANK // BLOCK // 2))


def second_half_kernel(half, after, a):
    a[...] = half[...]
    eliminate(a, range(RANK // BLOCK // 2, RANK // BLOCK))
    row = lax.broadcasted_iota(jnp.int32, (RANK, RANK), 0)
    col = lax.broadcasted_iota(jnp.int32, (RANK, RANK), 1)
    a[...] = jnp.where(col <= row, a[...], 0.0)


def squares_kernel(column_mine, inverse, after, factor_mine, squares):
    c = dot(column_mine[...], inverse[...], 1, 1)
    factor_mine[...] = c
    squares[...] = jnp.sum(c * c, axis=0, keepdims=True)


def ortho_kernel(power, inverse, row_factor, weights):
    o = dot(power[...], inverse[...], 1, 1)
    row_factor[...] = o * math.sqrt(ROWS)
    weights[...] = 0.05 * dot(o, inverse[...], 1, 0)


def new_right_kernel(pieces, factor_mine, after, out):
    squares = jnp.sum(pieces[...], axis=0)
    out[...] = factor_mine[...] / jnp.sqrt(squares / COLS + 1e-06)


def split(value):
    high = value.astype(bf16)
    return high, (value - high.astype(f32)).astype(bf16)


def momentum_kernel(where, own, other, weights, mom, grad, out, token, mom_here, grad_here, full, sems, done):
    copies = []
    for j in range(STEPS):
        copies.append(
            factor_copies(where[0], own, other, full, sems, j)
            + buffer_copies(mom, grad, mom_here, grad_here, sems, j)
        )
        for copy in copies[j]:
            copy.start()
    high, low = split(weights[...])
    token[...] = jnp.zeros_like(token)
    for j in range(STEPS):
        for copy in copies[j]:
            copy.wait()
        fh, fl = split(full[pl.ds(j * SOME, SOME)].reshape(CHUNK, RANK))
        change = dot(high, fh, 1, 1, None) + (dot(high, fl, 1, 1, None) + dot(low, fh, 1, 1, None))
        cols = pl.ds(j * CHUNK, CHUNK)
        mom_here[:, cols] = buffer_chunk(mom_here, grad_here, j) - change
        copies[j] = pltpu.make_async_copy(mom_here.at[:, cols], out.at[:, cols], done.at[j])
        copies[j].start()
    for j in range(STEPS):
        copies[j].wait()


def spread(value, axis, size):
    copies = jnp.broadcast_to(value[None], (size,) + value.shape)
    return swap(copies, axis)


def swap(pieces, axis):
    return lax.all_to_all(pieces, axis, 0, 0)


def other_core(value):
    return lax.ppermute(value, "c", [(0, 1), (1, 0)])


def shards(momentum, gradient, right_factor):
    where = lax.axis_index("c").astype(jnp.int32).reshape(1)
    momentum = pltpu.with_memory_space_constraint(momentum, pltpu.HBM)
    gradient = pltpu.with_memory_space_constraint(gradient, pltpu.HBM)
    fsdp = ("x", "z", "c")

    own = spread(spread(right_factor, "z", NZ), "x", NX).reshape(CHIPS, SHARD, RANK)
    partial_power = call(
        power_kernel, shape(MY_ROWS, RANK), [SMEM] + [HBM] * 4,
        BUFFER_SCRATCH + FULL + SEMS, None, 12 * MACS, 7_000_000,
    )(where, own, other_core(own), momentum, gradient)

    pieces = swap(partial_power.reshape(NY, MY_ROWS // NY, RANK), "y")
    copies = call(sum_spread_kernel, shape(NY, MY_ROWS // NY, RANK), [VMEM])(pieces)
    power = swap(copies, "y").reshape(MY_ROWS, RANK)

    gram, token = call(gram_kernel, [shape(64, 8, 128), TOKEN], [VMEM])(power)
    gram_pieces = swap(gram, fsdp)
    keep, send = call(
        column_kernel, [in_hbm(CHIPS, SHARD, RANK)] * 2, [SMEM, VMEM, HBM, HBM, ANY],
        BUFFER_SCRATCH + SEMS + [pltpu.VMEM((CHIPS, SHARD, RANK), f32)] * 2,
        [HBM, HBM], 12 * MACS, 7_000_000,
    )(where, power, momentum, gradient, token)
    gram = call(sum_spread_kernel, shape(64, 8, 128), [VMEM])(gram_pieces)
    send, gram = lax.optimization_barrier((send, gram))
    arrived = other_core(send)
    block = pl.BlockSpec((SOME, SHARD, RANK), lambda i: (i, 0, 0))
    sums, token = pl.pallas_call(
        add_kernel,
        out_shape=[in_hbm(CHIPS, SHARD, RANK), TOKEN],
        grid=(STEPS,),
        in_specs=[block, block, ANY],
        out_specs=[block, pl.BlockSpec((8, 128), lambda i: (0, 0))],
        compiler_params=pltpu.CompilerParams(vmem_limit_bytes=8 * 2**20),
        cost_estimate=pl.CostEstimate(
            flops=1_000_000, bytes_accessed=6_000_000, transcendentals=0
        ),
    )(pltpu.with_memory_space_constraint(keep, pltpu.HBM), arrived, gram)
    gram = swap(gram, fsdp)

    by_x = swap(sums.reshape(NX, NZ, SHARD, RANK), "x")
    half = call(
        first_half_kernel, shape(RANK, RANK), [VMEM, ANY], flops=15_000_000_000
    )(gram, token)
    by_z, token = call(
        sum_kernel, [shape(NZ, SHARD, RANK), TOKEN], [VMEM, ANY], nbytes=3_000_000
    )(by_x, half)
    swapped = swap(by_z, "z")
    inverse = call(
        second_half_kernel, shape(RANK, RANK), [VMEM, ANY], flops=15_000_000_000
    )(half, token)
    column_mine, copies = call(
        column_mine_kernel, [shape(SHARD, RANK), shape(NZ, SHARD, RANK)], [VMEM, ANY]
    )(swapped, inverse)

    gathered = swap(copies, "z")
    factor_mine, squares = call(
        squares_kernel, [shape(SHARD, RANK), shape(1, RANK)], [VMEM, VMEM, ANY]
    )(column_mine, inverse, copies)
    for bit in (1, 2, 4):
        squares = squares + lax.ppermute(squares, "y", [(i, i ^ bit) for i in range(NY)])
    squares = jnp.broadcast_to(squares[None], (64, 1, RANK))
    copies = call(
        copies_kernel, shape(NX, NZ, SHARD, RANK), [VMEM, ANY], nbytes=3_000_000
    )(gathered, squares)
    own = swap(copies, "x").reshape(CHIPS, SHARD, RANK)
    row_factor, weights = call(
        ortho_kernel, [shape(MY_ROWS, RANK)] * 2, [VMEM, VMEM]
    )(power, inverse)
    squares = swap(squares, fsdp)
    new_momentum, token = call(
        momentum_kernel, [in_hbm(MY_ROWS, MY_COLS), TOKEN], [SMEM, HBM, HBM, VMEM, HBM, HBM],
        BUFFER_SCRATCH + FULL + SEMS + [pltpu.SemaphoreType.DMA((STEPS,))],
        [HBM, VMEM], 6 * MACS, 9_000_000,
    )(where, own, other_core(own), weights, momentum, gradient)
    new_right = call(
        new_right_kernel, shape(SHARD, RANK), [VMEM, VMEM, ANY]
    )(squares, factor_mine, token)
    return (new_momentum, new_right, row_factor)


def solution(mesh):
    devices = np.asarray(mesh.devices).reshape(NX, NZ, NC, NY)
    grid = Mesh(devices, ("x", "z", "c", "y"))
    fsdp = ("x", "z", "c")
    return jax.shard_map(
        shards,
        mesh=grid,
        in_specs=(P(fsdp, "y"), P(fsdp, "y"), P(("y",) + fsdp, None)),
        out_specs=(P(fsdp, "y"), P(("y",) + fsdp, None), P(fsdp, None)),
        check_vma=False,
    )
```

```python
import math

import jax
import jax.numpy as jnp
import numpy as np
from jax import lax
from jax.experimental import pallas as pl
from jax.experimental.pallas import tpu as pltpu
from jax.sharding import Mesh, PartitionSpec as P

ROWS = 8192
COLS = 28672
RANK = 256
NX, NZ, NC, NY = 4, 8, 2, 8
MY_ROWS = 128
MY_COLS = 3584
SHARD = 56
CHUNK = NZ * NC * SHARD
BLOCK = 32
MACS = MY_ROWS * MY_COLS * RANK

highest = lax.Precision.HIGHEST
f32 = jnp.float32
bf16 = jnp.bfloat16
VMEM = pl.BlockSpec(memory_space=pltpu.VMEM)
SMEM = pl.BlockSpec(memory_space=pltpu.SMEM)
ANY = pl.BlockSpec(memory_space=pl.ANY)
HBM = pl.BlockSpec(memory_space=pltpu.HBM)


def dot(a, b, ca, cb, precision=highest):
    return lax.dot_general(
        a, b, (((ca,), (cb,)), ((), ())), precision=precision, preferred_element_type=f32
    )


def shape(*dims):
    return jax.ShapeDtypeStruct(dims, f32)


def in_hbm(*dims):
    return pltpu.HBM(dims, f32)


TOKEN = shape(8, 128)


def call(kernel, out_shape, in_specs, scratch=(), out_specs=None, flops=1_000_000, nbytes=100_000, limit=12):
    return pl.pallas_call(
        kernel,
        out_shape=out_shape,
        in_specs=in_specs,
        out_specs=out_specs or jax.tree.map(lambda _: VMEM, out_shape),
        scratch_shapes=scratch,
        compiler_params=pltpu.CompilerParams(vmem_limit_bytes=limit * 2**20),
        cost_estimate=pl.CostEstimate(
            flops=flops, bytes_accessed=nbytes, transcendentals=0
        ),
    )


def columns(x, dx):
    return pl.ds(pl.multiple_of(lax.rem(x - dx + NX, NX) * CHUNK, 128), CHUNK)


def buffer_copies(cols, mom, grad, mom_here, grad_here, sems, j):
    return [
        pltpu.make_async_copy(mom.at[:, cols], mom_here.at[:, cols], sems.at[j, 0]),
        pltpu.make_async_copy(grad.at[:, cols], grad_here.at[:, cols], sems.at[j, 1]),
    ]


def factor_copies(core, own, other, full, sems, j):
    return [
        pltpu.make_async_copy(own, full.at[j, :, core], sems.at[j, 2]),
        pltpu.make_async_copy(other, full.at[j, :, 1 - core], sems.at[j, 3]),
    ]


def gathered_copies(where, pieces, mom, grad, mom_here, grad_here, full, sems):
    copies = []
    for j in range(NX):
        copies.append(
            factor_copies(where[1], pieces[j], pieces[NX + j], full, sems, j)
            + buffer_copies(columns(where[0], j), mom, grad, mom_here, grad_here, sems, j)
        )
        for copy in copies[j]:
            copy.start()
    return copies


def buffer_chunk(mom, grad, cols):
    return mom[:, cols] + grad[:, cols].astype(f32)


BUFFER_SCRATCH = [pltpu.VMEM((MY_ROWS, MY_COLS), f32), pltpu.VMEM((MY_ROWS, MY_COLS), bf16)]
SEMS = [pltpu.SemaphoreType.DMA((NX, 4))]
FULL = [pltpu.VMEM((NX, NZ, NC, SHARD, RANK), f32)]


def power_kernel(where, *refs):
    pieces, (mom, grad, out, mom_here, grad_here, full, sems) = refs[:8], refs[8:]
    copies = gathered_copies(where, pieces, mom, grad, mom_here, grad_here, full, sems)
    total = None
    for j in range(NX):
        for copy in copies[j]:
            copy.wait()
        part = full[j].reshape(CHUNK, RANK)
        part = dot(buffer_chunk(mom_here, grad_here, columns(where[0], j)), part, 1, 0)
        total = part if total is None else total + part
    out[...] = total


def sum_spread_kernel(pieces, out):
    total = jnp.sum(pieces[...], axis=0)
    for i in range(out.shape[0]):
        out[i] = total


def gram_kernel(power, out, token):
    token[...] = jnp.zeros_like(token)
    gram = dot(power[...], power[...], 0, 0)
    for i in range(RANK // 8):
        for h in range(RANK // 128):
            out[i * 2 + h] = gram[i * 8 : i * 8 + 8, h * 128 : h * 128 + 128]


def column_kernel(where, power, mom, grad, after, keep, send, mom_here, grad_here, full, sems):
    copies = []
    for j in range(NX):
        copies.append(
            buffer_copies(columns(where[0], -j), mom, grad, mom_here, grad_here, sems, j)
        )
        for copy in copies[j]:
            copy.start()
    for j in range(NX):
        for copy in copies[j]:
            copy.wait()
        part = dot(buffer_chunk(mom_here, grad_here, columns(where[0], -j)), power[...], 0, 0)
        full[j] = part.reshape(NZ, NC, SHARD, RANK)
        copies[j] = [
            pltpu.make_async_copy(full.at[j, :, 1 - where[1]], send.at[j], sems.at[j, 2]),
            pltpu.make_async_copy(full.at[j, :, where[1]], keep.at[j], sems.at[j, 3]),
        ]
        for copy in copies[j]:
            copy.start()
    for j in range(NX):
        for copy in copies[j]:
            copy.wait()


def sum_kernel(a, b, c, d, after, out, token):
    token[...] = jnp.zeros_like(token)
    out[...] = (a[...] + b[...]) + (c[...] + d[...])


def column_mine_kernel(pieces, after, mine, copies):
    total = jnp.sum(pieces[...], axis=0)
    mine[...] = total
    for i in range(NZ):
        copies[i] = total


def eliminate(a, blocks):
    row = lax.broadcasted_iota(jnp.int32, (BLOCK, BLOCK), 0)
    col = lax.broadcasted_iota(jnp.int32, (BLOCK, BLOCK), 1)
    eye = (row == col).astype(f32)
    wide = lax.broadcasted_iota(jnp.int32, (BLOCK, RANK), 1)
    for k in blocks:
        lo, hi = k * BLOCK, (k + 1) * BLOCK
        d = a[lo:hi, lo:hi]
        for j in range(BLOCK - 1):
            column = jnp.broadcast_to(d[:, j : j + 1], (BLOCK, BLOCK))
            pivot = jnp.broadcast_to(1.0 / column[j : j + 1, :], (BLOCK, BLOCK))
            line = jnp.broadcast_to(d[j : j + 1, :], (BLOCK, BLOCK))
            line = jnp.where(col == j, 1.0, line)
            rest = jnp.where(col == j, 0.0, d)
            d = jnp.where(row > j, rest - column * (line * pivot), d)
        diagonal = jnp.sum(d * eye, axis=1, keepdims=True)
        inner = (jnp.where(row > col, d, 0.0) + eye) * lax.rsqrt(diagonal)
        panel = a[lo:hi, :]
        panel = jnp.where((wide >= lo) & (wide < hi), 0.0, panel)
        panel = dot(inner, panel, 1, 0)
        a[lo:hi, :] = panel
        a[lo:hi, lo:hi] = inner
        panel = a[lo:hi, :]
        if hi < RANK:
            change = dot(panel, panel, 0, 0)
            a[hi:, lo:hi] = jnp.zeros((RANK - hi, BLOCK), f32)
            a[hi:, :] = a[hi:, :] - change[hi:, :]


def first_half_kernel(gram, a):
    for i in range(RANK // 8):
        for h in range(RANK // 128):
            a[i * 8 : i * 8 + 8, h * 128 : h * 128 + 128] = gram[i * 2 + h]
    eliminate(a, range(0, RANK // BLOCK // 2))


def second_half_kernel(half, after, a):
    a[...] = half[...]
    eliminate(a, range(RANK // BLOCK // 2, RANK // BLOCK))
    row = lax.broadcasted_iota(jnp.int32, (RANK, RANK), 0)
    col = lax.broadcasted_iota(jnp.int32, (RANK, RANK), 1)
    a[...] = jnp.where(col <= row, a[...], 0.0)


def squares_kernel(column_mine, inverse, after, factor_mine, squares):
    c = dot(column_mine[...], inverse[...], 1, 1)
    factor_mine[...] = c
    squares[...] = jnp.sum(c * c, axis=0, keepdims=True)


def ortho_kernel(power, inverse, row_factor, weights):
    o = dot(power[...], inverse[...], 1, 1)
    row_factor[...] = o * math.sqrt(ROWS)
    weights[...] = 0.05 * dot(o, inverse[...], 1, 0)


def new_right_kernel(pieces, factor_mine, out):
    squares = jnp.sum(pieces[...], axis=0)
    out[...] = factor_mine[...] / jnp.sqrt(squares / COLS + 1e-06)


def split(value):
    high = value.astype(bf16)
    return high, (value - high.astype(f32)).astype(bf16)


def momentum_kernel(where, *refs):
    pieces, (weights, mom, grad, out, mom_here, grad_here, full, sems, done) = refs[:8], refs[8:]
    copies = gathered_copies(where, pieces, mom, grad, mom_here, grad_here, full, sems)
    high, low = split(weights[...])
    for j in range(NX):
        for copy in copies[j]:
            copy.wait()
        fh, fl = split(full[j].reshape(CHUNK, RANK))
        change = dot(high, fh, 1, 1, None) + (dot(high, fl, 1, 1, None) + dot(low, fh, 1, 1, None))
        cols = columns(where[0], j)
        mom_here[:, cols] = buffer_chunk(mom_here, grad_here, cols) - change
        copies[j] = pltpu.make_async_copy(mom_here.at[:, cols], out.at[:, cols], done.at[j])
        copies[j].start()
    for j in range(NX):
        copies[j].wait()


def spread(value, axis, size):
    copies = jnp.broadcast_to(value[None], (size,) + value.shape)
    return swap(copies, axis)


def swap(pieces, axis):
    return lax.all_to_all(pieces, axis, 0, 0)


def other_core(value):
    return lax.ppermute(value, "c", [(0, 1), (1, 0)])


def shift(value, by):
    return lax.ppermute(value, "x", [(i, (i + by) % NX) for i in range(NX)])


def gather_rest(block):
    own = [block] + [shift(block, d) for d in (1, 2, 3)]
    return own + [other_core(piece) for piece in own]


def shards(momentum, gradient, right_factor):
    where = jnp.stack([lax.axis_index("x"), lax.axis_index("c")]).astype(jnp.int32)
    momentum = pltpu.with_memory_space_constraint(momentum, pltpu.HBM)
    gradient = pltpu.with_memory_space_constraint(gradient, pltpu.HBM)
    fsdp = ("x", "z", "c")

    pieces = gather_rest(spread(right_factor, "z", NZ))
    partial_power = call(
        power_kernel, shape(MY_ROWS, RANK), [SMEM] + [HBM] * 10,
        BUFFER_SCRATCH + FULL + SEMS, None, 12 * MACS, 7_000_000,
    )(where, *pieces, momentum, gradient)

    pieces = swap(partial_power.reshape(NY, MY_ROWS // NY, RANK), "y")
    copies = call(sum_spread_kernel, shape(NY, MY_ROWS // NY, RANK), [VMEM])(pieces)
    power = swap(copies, "y").reshape(MY_ROWS, RANK)

    gram, token = call(gram_kernel, [shape(64, 8, 128), TOKEN], [VMEM])(power)
    gram = swap(gram, fsdp)
    keep, send = call(
        column_kernel, [in_hbm(NX, NZ, SHARD, RANK)] * 2, [SMEM, VMEM, HBM, HBM, ANY],
        BUFFER_SCRATCH + FULL + SEMS, [HBM, HBM], 12 * MACS, 7_000_000,
    )(where, power, momentum, gradient, token)
    gram = call(sum_spread_kernel, shape(64, 8, 128), [VMEM])(gram)
    send, gram = lax.optimization_barrier((send, gram))
    arrived = other_core(send)
    sums = [keep[d] + arrived[d] for d in range(NX)]
    gram, *sums[1:] = lax.optimization_barrier((gram, *sums[1:]))
    parts = [sums[0]] + [shift(sums[d], d) for d in (1, 2, 3)]
    half = call(first_half_kernel, shape(RANK, RANK), [VMEM], flops=15_000_000_000)(
        swap(gram, fsdp)
    )
    by_z, token = call(
        sum_kernel, [shape(NZ, SHARD, RANK), TOKEN], [VMEM] * 4 + [ANY], nbytes=3_000_000
    )(*parts, half)
    swapped = swap(by_z, "z")
    inverse = call(
        second_half_kernel, shape(RANK, RANK), [VMEM, ANY], flops=15_000_000_000
    )(half, token)
    column_mine, copies = call(
        column_mine_kernel, [shape(SHARD, RANK), shape(NZ, SHARD, RANK)], [VMEM, ANY]
    )(swapped, inverse)

    gathered = swap(copies, "z")
    factor_mine, squares = call(
        squares_kernel, [shape(SHARD, RANK), shape(1, RANK)], [VMEM, VMEM, ANY]
    )(column_mine, inverse, copies)
    squares = squares + other_core(squares)
    for bit in (1, 2):
        squares = squares + lax.ppermute(squares, "x", [(i, i ^ bit) for i in range(NX)])
    row_factor, weights = call(
        ortho_kernel, [shape(MY_ROWS, RANK)] * 2, [VMEM, VMEM]
    )(power, inverse)
    gathered, squares, weights = lax.optimization_barrier((gathered, squares, weights))
    squares = swap(jnp.broadcast_to(squares[None], (64, 1, RANK)), ("z", "y"))
    own = [gathered] + [shift(gathered, d) for d in (1, 2, 3)]
    squares, *own[1:] = lax.optimization_barrier((squares, *own[1:]))
    pieces = own + [other_core(piece) for piece in own]
    new_right = call(new_right_kernel, shape(SHARD, RANK), [VMEM, VMEM])(squares, factor_mine)
    new_momentum = call(
        momentum_kernel, in_hbm(MY_ROWS, MY_COLS), [SMEM] + [HBM] * 8 + [VMEM, HBM, HBM],
        BUFFER_SCRATCH + FULL + SEMS + [pltpu.SemaphoreType.DMA((NX,))],
        HBM, 6 * MACS, 9_000_000,
    )(where, *pieces, weights, momentum, gradient)
    return (new_momentum, new_right, row_factor)


def solution(mesh):
    devices = np.asarray(mesh.devices).reshape(NX, NZ, NC, NY)
    grid = Mesh(devices, ("x", "z", "c", "y"))
    fsdp = ("x", "z", "c")
    return jax.shard_map(
        shards,
        mesh=grid,
        in_specs=(P(fsdp, "y"), P(fsdp, "y"), P(("y",) + fsdp, None)),
        out_specs=(P(fsdp, "y"), P(("y",) + fsdp, None), P(fsdp, None)),
        check_vma=False,
    )
```

```python
import math

import jax
import jax.numpy as jnp
import numpy as np
from jax import lax
from jax.experimental import pallas as pl
from jax.experimental.pallas import tpu as pltpu
from jax.sharding import Mesh, PartitionSpec as P

ROWS = 8192
COLS = 28672
RANK = 256
NX, NZ, NC, NY = 4, 8, 2, 8
MY_ROWS = 128
MY_COLS = 3584
SHARD = 56
CHUNK = NZ * NC * SHARD
HALF = 128
GROUP = 8
PER_SHARD = SHARD // GROUP
PER_X = NZ * PER_SHARD
MACS = MY_ROWS * MY_COLS * RANK

highest = lax.Precision.HIGHEST
f32 = jnp.float32
bf16 = jnp.bfloat16
VMEM = pl.BlockSpec(memory_space=pltpu.VMEM)
SMEM = pl.BlockSpec(memory_space=pltpu.SMEM)
ANY = pl.BlockSpec(memory_space=pl.ANY)
HBM = pl.BlockSpec(memory_space=pltpu.HBM)


def dot(a, b, ca, cb, precision=highest):
    return lax.dot_general(
        a, b, (((ca,), (cb,)), ((), ())), precision=precision, preferred_element_type=f32
    )


def shape(*dims):
    return jax.ShapeDtypeStruct(dims, f32)


def in_hbm(*dims):
    return pltpu.HBM(dims, f32)


TOKEN = shape(8, 128)


def call(kernel, out_shape, in_specs, scratch=(), out_specs=None, flops=1_000_000, nbytes=100_000, limit=12):
    return pl.pallas_call(
        kernel,
        out_shape=out_shape,
        in_specs=in_specs,
        out_specs=out_specs or jax.tree.map(lambda _: VMEM, out_shape),
        scratch_shapes=scratch,
        compiler_params=pltpu.CompilerParams(vmem_limit_bytes=limit * 2**20),
        cost_estimate=pl.CostEstimate(
            flops=flops, bytes_accessed=nbytes, transcendentals=0
        ),
    )


def columns(j):
    return pl.ds(j * CHUNK, CHUNK)


def buffer_copies(mom, grad, mom_here, grad_here, sems, j):
    cols = columns(j)
    return [
        pltpu.make_async_copy(mom.at[:, cols], mom_here.at[:, cols], sems.at[j, 0]),
        pltpu.make_async_copy(grad.at[:, cols], grad_here.at[:, cols], sems.at[j, 1]),
    ]


def gathered_copies(where, own, other, mom, grad, mom_here, grad_here, full, sems):
    core = where[1]
    copies = []
    for j in range(NX):
        copies.append(
            [
                pltpu.make_async_copy(own.at[j], full.at[j, :, core], sems.at[j, 2]),
                pltpu.make_async_copy(other.at[j], full.at[j, :, 1 - core], sems.at[j, 3]),
            ]
            + buffer_copies(mom, grad, mom_here, grad_here, sems, j)
        )
        for copy in copies[j]:
            copy.start()
    return copies


def buffer_chunk(mom, grad, j):
    return mom[:, columns(j)] + grad[:, columns(j)].astype(f32)


BUFFER_SCRATCH = [pltpu.VMEM((MY_ROWS, MY_COLS), f32), pltpu.VMEM((MY_ROWS, MY_COLS), bf16)]
SEMS = [pltpu.SemaphoreType.DMA((NX, 4))]
FULL = [pltpu.VMEM((NX, NZ, NC, SHARD, RANK), f32)]


def power_kernel(where, own, other, mom, grad, out, mom_here, grad_here, full, sems):
    copies = gathered_copies(where, own, other, mom, grad, mom_here, grad_here, full, sems)
    total = None
    for j in range(NX):
        for copy in copies[j]:
            copy.wait()
        part = dot(buffer_chunk(mom_here, grad_here, j), full[j].reshape(CHUNK, RANK), 1, 0)
        total = part if total is None else total + part
    out[...] = total


def sum_spread_kernel(pieces, out):
    total = jnp.sum(pieces[...], axis=0)
    for i in range(out.shape[0]):
        out[i] = total


def column_kernel(where, power, mom, grad, keep, send, mom_here, grad_here, full, gram, sems, outs):
    copies = []
    for j in range(NX):
        copies.append(buffer_copies(mom, grad, mom_here, grad_here, sems, j))
        for copy in copies[j]:
            copy.start()
    gram[...] = dot(power[...], power[...], 0, 0).reshape(RANK // GROUP, GROUP, RANK)
    core = where[1]
    waits = []
    for j in range(NX):
        for copy in copies[j]:
            copy.wait()
        for q in range(CHUNK // HALF):
            cols = pl.ds(j * CHUNK + q * HALF, HALF)
            part = mom_here[:, cols] + grad_here[:, cols].astype(f32)
            part = dot(part, power[...], 0, 0)
            full[pl.ds((j * CHUNK + q * HALF) // GROUP, HALF // GROUP)] = part.reshape(
                HALF // GROUP, GROUP, RANK
            )
        for side, (out, c) in enumerate(((send, 1 - core), (keep, core))):
            for z in range(NZ):
                start = ((j * NZ + z) * NC + c) * PER_SHARD
                waits.append(
                    pltpu.make_async_copy(
                        full.at[pl.ds(start, PER_SHARD)],
                        out.at[j, pl.ds(z * PER_SHARD, PER_SHARD)],
                        outs.at[j, z, side],
                    )
                )
            waits.append(
                pltpu.make_async_copy(
                    gram.at[pl.ds(where[2] * NX + j, 1)],
                    out.at[j, pl.ds(PER_X, 1)],
                    outs.at[j, NZ, side],
                )
            )
        for copy in waits[-2 * (NZ + 1) :]:
            copy.start()
    for copy in waits:
        copy.wait()


def sum_x_kernel(pieces, out):
    total = (pieces[0] + pieces[1]) + (pieces[2] + pieces[3])
    for z in range(NZ):
        out[z, 0:PER_SHARD] = total[z * PER_SHARD : (z + 1) * PER_SHARD]
        out[z, PER_SHARD] = total[PER_X]


def sum_z_kernel(pieces, mine, copies, gram):
    total = jnp.sum(pieces[...], axis=0)
    column = total[0:PER_SHARD].reshape(SHARD, RANK)
    mine[...] = column
    for i in range(NZ):
        copies[i] = column
    for i in range(NX * NY):
        gram[i] = total[PER_SHARD]


def copies_kernel(value, after, out):
    for i in range(out.shape[0]):
        out[i] = value[...]


def inverse_factor(d):
    row = lax.broadcasted_iota(jnp.int32, (GROUP, HALF), 0)
    col = lax.broadcasted_iota(jnp.int32, (GROUP, HALF), 1)
    groups = [d[g * GROUP : (g + 1) * GROUP] for g in range(HALF // GROUP)]
    for j in range(0, HALF - 2, 2):
        g0, i = divmod(j, GROUP)
        column0 = [None] * len(groups)
        column1 = [None] * len(groups)
        for g in range(g0, len(groups)):
            column0[g] = jnp.broadcast_to(groups[g][:, j : j + 1], (GROUP, HALF))
            column1[g] = jnp.broadcast_to(groups[g][:, j + 1 : j + 2], (GROUP, HALF))
        p = column0[g0][i : i + 1]
        b = column0[g0][i + 1 : i + 2]
        q = column1[g0][i + 1 : i + 2]
        over_p = 1.0 / p
        ratio = b * over_p
        over_q = 1.0 / (q - ratio * b)
        first, second = col[0:1] == j, col[0:1] == j + 1
        line0 = jnp.where(first, 1.0, jnp.where(second, 0.0, groups[g0][i : i + 1]))
        line1 = jnp.where(first, 0.0, jnp.where(second, 1.0, groups[g0][i + 1 : i + 2]))
        line1 = over_q * (line1 - ratio * line0)
        line0 = over_p * line0 - ratio * line1
        line0 = jnp.broadcast_to(line0, (GROUP, HALF))
        line1 = jnp.broadcast_to(line1, (GROUP, HALF))
        pivots = (col == j) | (col == j + 1)
        for g in range(g0, len(groups)):
            rest = jnp.where(pivots, 0.0, groups[g])
            rest = rest - column0[g] * line0 - column1[g] * line1
            groups[g] = jnp.where(row > i + 1, rest, groups[g]) if g == g0 else rest
    odd = row % 2 == 1
    for g in range(len(groups)):
        at = row + g * GROUP
        d = groups[g]
        diagonal = jnp.sum(jnp.where(col == at, d, 0.0), axis=1, keepdims=True)
        diagonal = jnp.broadcast_to(diagonal, (GROUP, HALF))
        below = jnp.sum(jnp.where(col == at - 1, d, 0.0), axis=1, keepdims=True)
        below = jnp.broadcast_to(below, (GROUP, HALF))
        ratio = jnp.where(odd, below / pltpu.roll(diagonal, 1, 0), 0.0)
        scale = lax.rsqrt(diagonal - ratio * below)
        unit = jnp.where(col == at, 1.0, jnp.where(col < at - at % 2, d, 0.0))
        groups[g] = scale * (unit - ratio * pltpu.roll(unit, 1, 0))
    return jnp.concatenate(groups, axis=0)


def first_half_kernel(gram, out):
    inner = inverse_factor(gram[0:HALF, 0:HALF])
    upper = dot(inner, gram[0:HALF, HALF:], 1, 0)
    out[0] = inner
    out[1] = gram[HALF:, HALF:] - dot(upper, upper, 0, 0)
    out[2] = -dot(upper, inner, 0, 0)


def second_half_kernel(half, out):
    inner = inverse_factor(half[1])
    out[0:HALF, 0:HALF] = half[0]
    out[0:HALF, HALF:] = jnp.zeros((HALF, HALF), f32)
    out[HALF:, 0:HALF] = dot(inner, half[2], 1, 0)
    out[HALF:, HALF:] = inner


def squares_kernel(own, column_mine, inverse, factor_mine, squares):
    factor_mine[...] = dot(column_mine[...], inverse[...], 1, 1)
    total = jnp.zeros((1, RANK), f32)
    for x in range(NX):
        c = dot(own[x].reshape(NZ * SHARD, RANK), inverse[...], 1, 1)
        total = total + jnp.sum(c * c, axis=0, keepdims=True)
    for i in range(NY * NC):
        squares[i] = total


def ortho_kernel(power, inverse, row_factor, weights):
    o = dot(power[...], inverse[...], 1, 1)
    row_factor[...] = o * math.sqrt(ROWS)
    weights[...] = 0.05 * dot(o, inverse[...], 1, 0)


def new_right_kernel(pieces, factor_mine, after, out):
    squares = jnp.sum(pieces[...], axis=0)
    out[...] = factor_mine[...] / jnp.sqrt(squares / COLS + 1e-06)


def split(value):
    high = value.astype(bf16)
    return high, (value - high.astype(f32)).astype(bf16)


def momentum_kernel(
    where, own, other, weights, mom, grad, out, token, mom_here, grad_here, full, sems, done
):
    copies = gathered_copies(where, own, other, mom, grad, mom_here, grad_here, full, sems)
    high, low = split(weights[...])
    token[...] = jnp.zeros_like(token)
    for j in range(NX):
        for copy in copies[j]:
            copy.wait()
        fh, fl = split(full[j].reshape(CHUNK, RANK))
        change = dot(high, fh, 1, 1, None) + (dot(high, fl, 1, 1, None) + dot(low, fh, 1, 1, None))
        mom_here[:, columns(j)] = buffer_chunk(mom_here, grad_here, j) - change
        copies[j] = pltpu.make_async_copy(
            mom_here.at[:, columns(j)], out.at[:, columns(j)], done.at[j]
        )
        copies[j].start()
    for j in range(NX):
        copies[j].wait()


def spread(value, axis, size):
    copies = jnp.broadcast_to(value[None], (size,) + value.shape)
    return swap(copies, axis)


def swap(pieces, axis):
    return lax.all_to_all(pieces, axis, 0, 0)


def other_core(value):
    return lax.ppermute(value, "c", [(0, 1), (1, 0)])


def shards(momentum, gradient, right_factor):
    where = jnp.stack([lax.axis_index(a) for a in ("x", "c", "y")]).astype(jnp.int32)
    momentum = pltpu.with_memory_space_constraint(momentum, pltpu.HBM)
    gradient = pltpu.with_memory_space_constraint(gradient, pltpu.HBM)

    own = spread(spread(right_factor, "z", NZ), "x", NX)
    partial_power = call(
        power_kernel, shape(MY_ROWS, RANK), [SMEM] + [HBM] * 4,
        BUFFER_SCRATCH + FULL + SEMS, None, 12 * MACS, 7_000_000,
    )(where, own, other_core(own), momentum, gradient)

    pieces = swap(partial_power.reshape(NY, MY_ROWS // NY, RANK), "y")
    copies = call(sum_spread_kernel, shape(NY, MY_ROWS // NY, RANK), [VMEM])(pieces)
    power = swap(copies, "y").reshape(MY_ROWS, RANK)

    keep, send = call(
        column_kernel, [in_hbm(NX, PER_X + 1, GROUP, RANK)] * 2, [SMEM, VMEM, HBM, HBM],
        BUFFER_SCRATCH
        + [pltpu.VMEM((MY_COLS // GROUP, GROUP, RANK), f32)]
        + [pltpu.VMEM((RANK // GROUP, GROUP, RANK), f32)]
        + [pltpu.SemaphoreType.DMA((NX, 2)), pltpu.SemaphoreType.DMA((NX, NZ + 1, 2))],
        [HBM, HBM], 12 * MACS, 7_000_000,
    )(where, power, momentum, gradient)
    by_x = swap(keep + other_core(send), "x")
    by_z = call(
        sum_x_kernel, shape(NZ, PER_SHARD + 1, GROUP, RANK), [VMEM], nbytes=3_000_000
    )(by_x)
    column_mine, copies, gram = call(
        sum_z_kernel,
        [shape(SHARD, RANK), shape(NZ, SHARD, RANK), shape(NX * NY, GROUP, RANK)],
        [VMEM],
    )(swap(by_z, "z"))

    gram = swap(gram, ("y", "x")).reshape(RANK, RANK)
    gram, copies = lax.optimization_barrier((gram, copies))
    half = call(first_half_kernel, shape(3, HALF, HALF), [VMEM], flops=10_000_000_000)(gram)
    copies = call(
        copies_kernel, shape(NX, NZ, SHARD, RANK), [VMEM, ANY], nbytes=3_000_000
    )(swap(copies, "z"), half)
    half, copies = lax.optimization_barrier((half, copies))
    inverse = call(second_half_kernel, shape(RANK, RANK), [VMEM], flops=10_000_000_000)(half)
    own = swap(copies, "x")
    own, inverse = lax.optimization_barrier((own, inverse))
    factor_mine, squares = call(
        squares_kernel, [shape(SHARD, RANK), shape(NY * NC, 1, RANK)], [VMEM] * 3, (), None,
        6 * MACS, 2_000_000,
    )(own, column_mine, inverse)
    squares = swap(squares, ("y", "c"))
    row_factor, weights = call(
        ortho_kernel, [shape(MY_ROWS, RANK)] * 2, [VMEM, VMEM]
    )(power, inverse)
    new_momentum, token = call(
        momentum_kernel, [in_hbm(MY_ROWS, MY_COLS), TOKEN], [SMEM, HBM, HBM, VMEM, HBM, HBM],
        BUFFER_SCRATCH + FULL + SEMS + [pltpu.SemaphoreType.DMA((NX,))],
        [HBM, VMEM], 6 * MACS, 9_000_000,
    )(where, own, other_core(own), weights, momentum, gradient)
    new_right = call(new_right_kernel, shape(SHARD, RANK), [VMEM, VMEM, ANY])(
        squares, factor_mine, token
    )
    return (new_momentum, new_right, row_factor)


def solution(mesh):
    devices = np.asarray(mesh.devices).reshape(NX, NZ, NC, NY)
    grid = Mesh(devices, ("x", "z", "c", "y"))
    fsdp = ("x", "z", "c")
    return jax.shard_map(
        shards,
        mesh=grid,
        in_specs=(P(fsdp, "y"), P(fsdp, "y"), P(("y",) + fsdp, None)),
        out_specs=(P(fsdp, "y"), P(("y",) + fsdp, None), P(fsdp, None)),
        check_vma=False,
    )
```

```python
import math

import jax
import jax.numpy as jnp
import numpy as np
from jax import lax
from jax.experimental import pallas as pl
from jax.experimental.pallas import tpu as pltpu
from jax.sharding import Mesh, PartitionSpec as P

ROWS = 8192
COLS = 28672
RANK = 256
NX, NZ, NC, NY = 4, 8, 2, 8
MY_ROWS = 128
MY_COLS = 3584
SHARD = 56
CHUNK = NZ * NC * SHARD
HALF = 128
GROUP = 8
PER_SHARD = SHARD // GROUP
PER_X = NZ * PER_SHARD
PER_CORE = MY_COLS // NC
MACS = MY_ROWS * MY_COLS * RANK

highest = lax.Precision.HIGHEST
f32 = jnp.float32
bf16 = jnp.bfloat16
VMEM = pl.BlockSpec(memory_space=pltpu.VMEM)
SMEM = pl.BlockSpec(memory_space=pltpu.SMEM)
ANY = pl.BlockSpec(memory_space=pl.ANY)
HBM = pl.BlockSpec(memory_space=pltpu.HBM)


def dot(a, b, ca, cb, precision=highest):
    return lax.dot_general(
        a, b, (((ca,), (cb,)), ((), ())), precision=precision, preferred_element_type=f32
    )


def shape(*dims):
    return jax.ShapeDtypeStruct(dims, f32)


def in_hbm(*dims):
    return pltpu.HBM(dims, f32)


TOKEN = shape(8, 128)


def call(kernel, out_shape, in_specs, scratch=(), out_specs=None, flops=1_000_000, nbytes=100_000, limit=12):
    return pl.pallas_call(
        kernel,
        out_shape=out_shape,
        in_specs=in_specs,
        out_specs=out_specs or jax.tree.map(lambda _: VMEM, out_shape),
        scratch_shapes=scratch,
        compiler_params=pltpu.CompilerParams(vmem_limit_bytes=limit * 2**20),
        cost_estimate=pl.CostEstimate(
            flops=flops, bytes_accessed=nbytes, transcendentals=0
        ),
    )


def columns(j):
    return pl.ds(j * CHUNK, CHUNK)


def buffer_copies(mom, grad, mom_here, grad_here, sems, j):
    cols = columns(j)
    return [
        pltpu.make_async_copy(mom.at[:, cols], mom_here.at[:, cols], sems.at[j, 0]),
        pltpu.make_async_copy(grad.at[:, cols], grad_here.at[:, cols], sems.at[j, 1]),
    ]


def gathered_copies(where, own, other, mom, grad, mom_here, grad_here, full, sems):
    core = where[1]
    copies = []
    for j in range(NX):
        copies.append(
            [
                pltpu.make_async_copy(own.at[j], full.at[j, :, core], sems.at[j, 2]),
                pltpu.make_async_copy(other.at[j], full.at[j, :, 1 - core], sems.at[j, 3]),
            ]
            + buffer_copies(mom, grad, mom_here, grad_here, sems, j)
        )
        for copy in copies[j]:
            copy.start()
    return copies


def buffer_chunk(mom, grad, j):
    return mom[:, columns(j)] + grad[:, columns(j)].astype(f32)


BUFFER_SCRATCH = [pltpu.VMEM((MY_ROWS, MY_COLS), f32), pltpu.VMEM((MY_ROWS, MY_COLS), bf16)]
SEMS = [pltpu.SemaphoreType.DMA((NX, 4))]
FULL = [pltpu.VMEM((NX, NZ, NC, SHARD, RANK), f32)]


def layout_kernel(where, mom, grad, own, other, own_t, other_t):
    first = where[1] == 0
    for j in range(NX):
        part = buffer_chunk(mom, grad, j).T.reshape(NZ, NC, SHARD, MY_ROWS)
        rows = pl.ds(j * NZ * SHARD, NZ * SHARD)
        own_t[rows] = jnp.where(first, part[:, 0], part[:, 1]).reshape(NZ * SHARD, MY_ROWS)
        other_t[rows] = jnp.where(first, part[:, 1], part[:, 0]).reshape(NZ * SHARD, MY_ROWS)
    for j in range(PER_CORE // CHUNK):
        own[:, columns(j)] = own_t[columns(j)].T
        other[:, columns(j)] = other_t[columns(j)].T


def own_power_kernel(buffer, factor, out):
    total = None
    for j in range(PER_CORE // CHUNK):
        part = factor[j * 2 : j * 2 + 2].reshape(CHUNK, RANK)
        part = dot(buffer[:, columns(j)], part, 1, 0)
        total = part if total is None else total + part
    out[...] = total


def power_kernel(buffer, factor, before, out, here, full, sems):
    copies = []
    for j in range(PER_CORE // CHUNK):
        pair = pl.ds(j * 2, 2)
        copies.append(
            [
                pltpu.make_async_copy(factor.at[pair], full.at[pair], sems.at[j, 0]),
                pltpu.make_async_copy(
                    buffer.at[:, columns(j)], here.at[:, columns(j)], sems.at[j, 1]
                ),
            ]
        )
        for copy in copies[j]:
            copy.start()
    total = before[...]
    for j in range(PER_CORE // CHUNK):
        for copy in copies[j]:
            copy.wait()
        part = full[j * 2 : j * 2 + 2].reshape(CHUNK, RANK)
        total = total + dot(here[:, columns(j)], part, 1, 0)
    out[...] = total


def sum_spread_kernel(pieces, out):
    total = jnp.sum(pieces[...], axis=0)
    for i in range(out.shape[0]):
        out[i] = total


def column_kernel(where, power, buffer_t, after, out, token, gram):
    token[...] = jnp.zeros_like(token)
    gram[...] = dot(power[...], power[...], 0, 0).reshape(RANK // GROUP, GROUP, RANK)
    for x in range(NX):
        part = dot(buffer_t[pl.ds(x * NZ * SHARD, NZ * SHARD)], power[...], 1, 0)
        out[x, 0:PER_X] = part.reshape(PER_X, GROUP, RANK)
        out[x, pl.ds(PER_X, 1)] = gram[pl.ds(where[2] * NX + x, 1)]


def sum_x_kernel(pieces, out):
    total = (pieces[0] + pieces[1]) + (pieces[2] + pieces[3])
    for z in range(NZ):
        out[z, 0:PER_SHARD] = total[z * PER_SHARD : (z + 1) * PER_SHARD]
        out[z, PER_SHARD] = total[PER_X]


def sum_z_kernel(pieces, mine, copies, gram):
    total = jnp.sum(pieces[...], axis=0)
    column = total[0:PER_SHARD].reshape(SHARD, RANK)
    mine[...] = column
    for i in range(NZ):
        copies[i] = column
    for i in range(NX * NY):
        gram[i] = total[PER_SHARD]


def copies_kernel(value, after, out):
    for i in range(out.shape[0]):
        out[i] = value[...]


def inverse_factor(d):
    row = lax.broadcasted_iota(jnp.int32, (GROUP, HALF), 0)
    col = lax.broadcasted_iota(jnp.int32, (GROUP, HALF), 1)
    groups = [d[g * GROUP : (g + 1) * GROUP] for g in range(HALF // GROUP)]
    for j in range(0, HALF - 2, 2):
        g0, i = divmod(j, GROUP)
        column0 = [None] * len(groups)
        column1 = [None] * len(groups)
        for g in range(g0, len(groups)):
            column0[g] = jnp.broadcast_to(groups[g][:, j : j + 1], (GROUP, HALF))
            column1[g] = jnp.broadcast_to(groups[g][:, j + 1 : j + 2], (GROUP, HALF))
        p = column0[g0][i : i + 1]
        b = column0[g0][i + 1 : i + 2]
        q = column1[g0][i + 1 : i + 2]
        over_p = 1.0 / p
        ratio = b * over_p
        over_q = 1.0 / (q - ratio * b)
        first, second = col[0:1] == j, col[0:1] == j + 1
        line0 = jnp.where(first, 1.0, jnp.where(second, 0.0, groups[g0][i : i + 1]))
        line1 = jnp.where(first, 0.0, jnp.where(second, 1.0, groups[g0][i + 1 : i + 2]))
        line1 = over_q * (line1 - ratio * line0)
        line0 = over_p * line0 - ratio * line1
        line0 = jnp.broadcast_to(line0, (GROUP, HALF))
        line1 = jnp.broadcast_to(line1, (GROUP, HALF))
        pivots = (col == j) | (col == j + 1)
        for g in range(g0, len(groups)):
            rest = jnp.where(pivots, 0.0, groups[g])
            rest = rest - column0[g] * line0 - column1[g] * line1
            groups[g] = jnp.where(row > i + 1, rest, groups[g]) if g == g0 else rest
    odd = row % 2 == 1
    for g in range(len(groups)):
        at = row + g * GROUP
        d = groups[g]
        diagonal = jnp.sum(jnp.where(col == at, d, 0.0), axis=1, keepdims=True)
        diagonal = jnp.broadcast_to(diagonal, (GROUP, HALF))
        below = jnp.sum(jnp.where(col == at - 1, d, 0.0), axis=1, keepdims=True)
        below = jnp.broadcast_to(below, (GROUP, HALF))
        ratio = jnp.where(odd, below / pltpu.roll(diagonal, 1, 0), 0.0)
        scale = lax.rsqrt(diagonal - ratio * below)
        unit = jnp.where(col == at, 1.0, jnp.where(col < at - at % 2, d, 0.0))
        groups[g] = scale * (unit - ratio * pltpu.roll(unit, 1, 0))
    return jnp.concatenate(groups, axis=0)


def first_half_kernel(gram, out):
    inner = inverse_factor(gram[0:HALF, 0:HALF])
    upper = dot(inner, gram[0:HALF, HALF:], 1, 0)
    out[0] = inner
    out[1] = gram[HALF:, HALF:] - dot(upper, upper, 0, 0)
    out[2] = -dot(upper, inner, 0, 0)


def second_half_kernel(half, out):
    inner = inverse_factor(half[1])
    out[0:HALF, 0:HALF] = half[0]
    out[0:HALF, HALF:] = jnp.zeros((HALF, HALF), f32)
    out[HALF:, 0:HALF] = dot(inner, half[2], 1, 0)
    out[HALF:, HALF:] = inner


def squares_kernel(gathered, column_mine, inverse, factor_mine, squares):
    factor_mine[...] = dot(column_mine[...], inverse[...], 1, 1)
    c = dot(gathered[...].reshape(NZ * SHARD, RANK), inverse[...], 1, 1)
    squares[...] = jnp.sum(c * c, axis=0, keepdims=True)


def ortho_kernel(power, inverse, row_factor, weights):
    o = dot(power[...], inverse[...], 1, 1)
    row_factor[...] = o * math.sqrt(ROWS)
    weights[...] = 0.05 * dot(o, inverse[...], 1, 0)


def new_right_kernel(pieces, factor_mine, after, out):
    squares = jnp.sum(pieces[...], axis=0)
    out[...] = factor_mine[...] / jnp.sqrt(squares / COLS + 1e-06)


def split(value):
    high = value.astype(bf16)
    return high, (value - high.astype(f32)).astype(bf16)


def momentum_kernel(
    where, own, other, weights, mom, grad, out, token, mom_here, grad_here, full, sems, done
):
    copies = gathered_copies(where, own, other, mom, grad, mom_here, grad_here, full, sems)
    high, low = split(weights[...])
    token[...] = jnp.zeros_like(token)
    for j in range(NX):
        for copy in copies[j]:
            copy.wait()
        fh, fl = split(full[j].reshape(CHUNK, RANK))
        change = dot(high, fh, 1, 1, None) + (dot(high, fl, 1, 1, None) + dot(low, fh, 1, 1, None))
        mom_here[:, columns(j)] = buffer_chunk(mom_here, grad_here, j) - change
        copies[j] = pltpu.make_async_copy(
            mom_here.at[:, columns(j)], out.at[:, columns(j)], done.at[j]
        )
        copies[j].start()
    for j in range(NX):
        copies[j].wait()


def spread(value, axis, size):
    copies = jnp.broadcast_to(value[None], (size,) + value.shape)
    return swap(copies, axis)


def swap(pieces, axis):
    return lax.all_to_all(pieces, axis, 0, 0)


def other_core(value):
    return lax.ppermute(value, "c", [(0, 1), (1, 0)])


def shards(momentum, gradient, right_factor):
    where = jnp.stack([lax.axis_index(a) for a in ("x", "c", "y")]).astype(jnp.int32)
    momentum = pltpu.with_memory_space_constraint(momentum, pltpu.HBM)
    gradient = pltpu.with_memory_space_constraint(gradient, pltpu.HBM)

    halves = [shape(MY_ROWS, PER_CORE)] * 2 + [shape(PER_CORE, MY_ROWS)] * 2
    by_core = call(
        layout_kernel, halves, [SMEM, VMEM, VMEM], (), None, 1_000_000_000, 9_000_000, 24
    )(where, momentum, gradient)
    gathered = spread(right_factor, "z", NZ)
    gathered, *by_core = lax.optimization_barrier((gathered, *by_core))
    buffer_own, buffer_other, own_t, other_t = by_core
    own = spread(gathered, "x", NX)
    own_power = call(
        own_power_kernel, shape(MY_ROWS, RANK), [VMEM, VMEM], (), None, 6 * MACS, 3_000_000
    )(buffer_own, own)
    partial_power = call(
        power_kernel, shape(MY_ROWS, RANK), [HBM, HBM, VMEM],
        [
            pltpu.VMEM((MY_ROWS, PER_CORE), f32),
            pltpu.VMEM((NX, NZ, SHARD, RANK), f32),
            pltpu.SemaphoreType.DMA((PER_CORE // CHUNK, 2)),
        ],
        None, 6 * MACS, 3_000_000,
    )(buffer_other, other_core(own), own_power)

    pieces = swap(partial_power.reshape(NY, MY_ROWS // NY, RANK), "y")
    copies = call(sum_spread_kernel, shape(NY, MY_ROWS // NY, RANK), [VMEM])(pieces)
    power = swap(copies, "y").reshape(MY_ROWS, RANK)

    def columns_of(buffer_t, after):
        return call(
            column_kernel, [shape(NX, PER_X + 1, GROUP, RANK), TOKEN], [SMEM, VMEM, VMEM, ANY],
            [pltpu.VMEM((RANK // GROUP, GROUP, RANK), f32)], None, 6 * MACS, 3_000_000,
        )(where, power, buffer_t, after)

    send, token = columns_of(other_t, where)
    arrived = other_core(send)
    keep, token = columns_of(own_t, token)
    by_x = swap(keep + arrived, "x")
    by_z = call(
        sum_x_kernel, shape(NZ, PER_SHARD + 1, GROUP, RANK), [VMEM], nbytes=3_000_000
    )(by_x)
    column_mine, copies, gram = call(
        sum_z_kernel,
        [shape(SHARD, RANK), shape(NZ, SHARD, RANK), shape(NX * NY, GROUP, RANK)],
        [VMEM],
    )(swap(by_z, "z"))

    gram = swap(gram, ("y", "x")).reshape(RANK, RANK)
    gram, copies = lax.optimization_barrier((gram, copies))
    half = call(first_half_kernel, shape(3, HALF, HALF), [VMEM], flops=10_000_000_000)(gram)
    gathered = swap(copies, "z")
    copies = call(
        copies_kernel, shape(NX, NZ, SHARD, RANK), [VMEM, ANY], nbytes=3_000_000
    )(gathered, half)
    half, copies = lax.optimization_barrier((half, copies))
    own = swap(copies, "x")
    inverse = call(second_half_kernel, shape(RANK, RANK), [VMEM], flops=10_000_000_000)(half)
    factor_mine, squares = call(
        squares_kernel, [shape(SHARD, RANK), shape(1, RANK)], [VMEM] * 3, (), None, 2 * MACS
    )(gathered, column_mine, inverse)
    for bit in (1, 2):
        squares = squares + lax.ppermute(squares, "x", [(i, i ^ bit) for i in range(NX)])
    row_factor, weights = call(
        ortho_kernel, [shape(MY_ROWS, RANK)] * 2, [VMEM, VMEM]
    )(power, inverse)
    own, squares, weights = lax.optimization_barrier((own, squares, weights))
    squares = swap(jnp.broadcast_to(squares[None], (NY * NC, 1, RANK)), ("y", "c"))
    new_momentum, token = call(
        momentum_kernel, [in_hbm(MY_ROWS, MY_COLS), TOKEN], [SMEM, HBM, HBM, VMEM, HBM, HBM],
        BUFFER_SCRATCH + FULL + SEMS + [pltpu.SemaphoreType.DMA((NX,))],
        [HBM, VMEM], 6 * MACS, 9_000_000,
    )(where, own, other_core(own), weights, momentum, gradient)
    new_right = call(new_right_kernel, shape(SHARD, RANK), [VMEM, VMEM, ANY])(
        squares, factor_mine, token
    )
    return (new_momentum, new_right, row_factor)


def solution(mesh):
    devices = np.asarray(mesh.devices).reshape(NX, NZ, NC, NY)
    grid = Mesh(devices, ("x", "z", "c", "y"))
    fsdp = ("x", "z", "c")
    return jax.shard_map(
        shards,
        mesh=grid,
        in_specs=(P(fsdp, "y"), P(fsdp, "y"), P(("y",) + fsdp, None)),
        out_specs=(P(fsdp, "y"), P(("y",) + fsdp, None), P(fsdp, None)),
        check_vma=False,
    )
```

```python
import math

import jax
import jax.numpy as jnp
import numpy as np
from jax import lax
from jax.experimental import pallas as pl
from jax.experimental.pallas import tpu as pltpu
from jax.sharding import Mesh, PartitionSpec as P

ROWS = 8192
COLS = 28672
RANK = 256
NX, NZ, NC, NY = 4, 8, 2, 8
MY_ROWS = 128
MY_COLS = 3584
SHARD = 56
CHUNK = NZ * NC * SHARD
HALF = 128
GROUP = 8
SOME = RANK // NY
PER_CORE = MY_COLS // NC
MACS = MY_ROWS * MY_COLS * RANK

highest = lax.Precision.HIGHEST
f32 = jnp.float32
bf16 = jnp.bfloat16
VMEM = pl.BlockSpec(memory_space=pltpu.VMEM)
SMEM = pl.BlockSpec(memory_space=pltpu.SMEM)
ANY = pl.BlockSpec(memory_space=pl.ANY)
HBM = pl.BlockSpec(memory_space=pltpu.HBM)


def dot(a, b, ca, cb, precision=highest):
    return lax.dot_general(
        a, b, (((ca,), (cb,)), ((), ())), precision=precision, preferred_element_type=f32
    )


def shape(*dims):
    return jax.ShapeDtypeStruct(dims, f32)


def in_hbm(*dims):
    return pltpu.HBM(dims, f32)


TOKEN = shape(8, 128)


def call(kernel, out_shape, in_specs, scratch=(), out_specs=None, flops=1_000_000, nbytes=100_000, limit=12):
    return pl.pallas_call(
        kernel,
        out_shape=out_shape,
        in_specs=in_specs,
        out_specs=out_specs or jax.tree.map(lambda _: VMEM, out_shape),
        scratch_shapes=scratch,
        compiler_params=pltpu.CompilerParams(vmem_limit_bytes=limit * 2**20),
        cost_estimate=pl.CostEstimate(
            flops=flops, bytes_accessed=nbytes, transcendentals=0
        ),
    )


def columns(j):
    return pl.ds(j * CHUNK, CHUNK)


def buffer_copies(mom, grad, mom_here, grad_here, sems, j):
    cols = columns(j)
    return [
        pltpu.make_async_copy(mom.at[:, cols], mom_here.at[:, cols], sems.at[j, 0]),
        pltpu.make_async_copy(grad.at[:, cols], grad_here.at[:, cols], sems.at[j, 1]),
    ]


def gathered_copies(where, own, other, mom, grad, mom_here, grad_here, full, sems):
    core = where[1]
    copies = []
    for j in range(NX):
        copies.append(
            [
                pltpu.make_async_copy(own.at[j], full.at[j, :, core], sems.at[j, 2]),
                pltpu.make_async_copy(other.at[j], full.at[j, :, 1 - core], sems.at[j, 3]),
            ]
            + buffer_copies(mom, grad, mom_here, grad_here, sems, j)
        )
        for copy in copies[j]:
            copy.start()
    return copies


def buffer_chunk(mom, grad, j):
    return mom[:, columns(j)] + grad[:, columns(j)].astype(f32)


BUFFER_SCRATCH = [pltpu.VMEM((MY_ROWS, MY_COLS), f32), pltpu.VMEM((MY_ROWS, MY_COLS), bf16)]
SEMS = [pltpu.SemaphoreType.DMA((NX, 4))]
FULL = [pltpu.VMEM((NX, NZ, NC, SHARD, RANK), f32)]


def layout_kernel(where, mom, grad, own, other, own_t, other_t):
    first = where[1] == 0
    for j in range(NX):
        part = buffer_chunk(mom, grad, j).T.reshape(NZ, NC, SHARD, MY_ROWS)
        rows = pl.ds(j * NZ * SHARD, NZ * SHARD)
        own_t[rows] = jnp.where(first, part[:, 0], part[:, 1]).reshape(NZ * SHARD, MY_ROWS)
        other_t[rows] = jnp.where(first, part[:, 1], part[:, 0]).reshape(NZ * SHARD, MY_ROWS)
    for j in range(PER_CORE // CHUNK):
        own[:, columns(j)] = own_t[columns(j)].T
        other[:, columns(j)] = other_t[columns(j)].T


def own_power_kernel(buffer, factor, out):
    total = None
    for j in range(PER_CORE // CHUNK):
        part = factor[j * 2 : j * 2 + 2].reshape(CHUNK, RANK)
        part = dot(buffer[:, columns(j)], part, 1, 0)
        total = part if total is None else total + part
    out[...] = total


def power_kernel(buffer, factor, before, out, here, full, sems):
    copies = []
    for j in range(PER_CORE // CHUNK):
        pair = pl.ds(j * 2, 2)
        copies.append(
            [
                pltpu.make_async_copy(factor.at[pair], full.at[pair], sems.at[j, 0]),
                pltpu.make_async_copy(
                    buffer.at[:, columns(j)], here.at[:, columns(j)], sems.at[j, 1]
                ),
            ]
        )
        for copy in copies[j]:
            copy.start()
    total = before[...]
    for j in range(PER_CORE // CHUNK):
        for copy in copies[j]:
            copy.wait()
        part = full[j * 2 : j * 2 + 2].reshape(CHUNK, RANK)
        total = total + dot(here[:, columns(j)], part, 1, 0)
    out[...] = total


def sum_spread_kernel(pieces, out):
    total = jnp.sum(pieces[...], axis=0)
    for i in range(out.shape[0]):
        out[i] = total


def column_product(power, buffer_t, out):
    for x in range(NX):
        part = dot(buffer_t[pl.ds(x * NZ * SHARD, NZ * SHARD)], power[...], 1, 0)
        out[x] = part.reshape(NZ, SHARD, RANK)


def send_kernel(where, power, buffer_t, out, some, gram):
    gram[...] = dot(power[...], power[...], 0, 0)
    some[...] = gram[pl.ds(pl.multiple_of(where[2] * SOME, 8), SOME), :]
    column_product(power, buffer_t, out)


def keep_kernel(power, buffer_t, after, out):
    column_product(power, buffer_t, out)


def sum_x_kernel(pieces, out):
    out[...] = (pieces[0] + pieces[1]) + (pieces[2] + pieces[3])


def sum_z_kernel(pieces, some, mine, copies, gram):
    column = jnp.sum(pieces[...], axis=0)
    mine[...] = column
    for i in range(NZ):
        copies[i] = column
    for i in range(NY):
        gram[i] = some[...]


def copies_kernel(value, after, out):
    for i in range(out.shape[0]):
        out[i] = value[...]


def inverse_factor(d):
    row = lax.broadcasted_iota(jnp.int32, (GROUP, HALF), 0)
    col = lax.broadcasted_iota(jnp.int32, (GROUP, HALF), 1)
    groups = [d[g * GROUP : (g + 1) * GROUP] for g in range(HALF // GROUP)]
    for j in range(0, HALF - 2, 2):
        g0, i = divmod(j, GROUP)
        column0 = [None] * len(groups)
        column1 = [None] * len(groups)
        for g in range(g0, len(groups)):
            column0[g] = jnp.broadcast_to(groups[g][:, j : j + 1], (GROUP, HALF))
            column1[g] = jnp.broadcast_to(groups[g][:, j + 1 : j + 2], (GROUP, HALF))
        p = column0[g0][i : i + 1]
        b = column0[g0][i + 1 : i + 2]
        q = column1[g0][i + 1 : i + 2]
        over_p = 1.0 / p
        ratio = b * over_p
        over_q = 1.0 / (q - ratio * b)
        first, second = col[0:1] == j, col[0:1] == j + 1
        line0 = jnp.where(first, 1.0, jnp.where(second, 0.0, groups[g0][i : i + 1]))
        line1 = jnp.where(first, 0.0, jnp.where(second, 1.0, groups[g0][i + 1 : i + 2]))
        line1 = over_q * (line1 - ratio * line0)
        line0 = over_p * line0 - ratio * line1
        line0 = jnp.broadcast_to(line0, (GROUP, HALF))
        line1 = jnp.broadcast_to(line1, (GROUP, HALF))
        pivots = (col == j) | (col == j + 1)
        for g in range(g0, len(groups)):
            rest = jnp.where(pivots, 0.0, groups[g])
            rest = rest - column0[g] * line0 - column1[g] * line1
            groups[g] = jnp.where(row > i + 1, rest, groups[g]) if g == g0 else rest
    odd = row % 2 == 1
    for g in range(len(groups)):
        at = row + g * GROUP
        d = groups[g]
        diagonal = jnp.sum(jnp.where(col == at, d, 0.0), axis=1, keepdims=True)
        diagonal = jnp.broadcast_to(diagonal, (GROUP, HALF))
        below = jnp.sum(jnp.where(col == at - 1, d, 0.0), axis=1, keepdims=True)
        below = jnp.broadcast_to(below, (GROUP, HALF))
        ratio = jnp.where(odd, below / pltpu.roll(diagonal, 1, 0), 0.0)
        scale = lax.rsqrt(diagonal - ratio * below)
        unit = jnp.where(col == at, 1.0, jnp.where(col < at - at % 2, d, 0.0))
        groups[g] = scale * (unit - ratio * pltpu.roll(unit, 1, 0))
    return jnp.concatenate(groups, axis=0)


def first_half_kernel(gram, out):
    inner = inverse_factor(gram[0:HALF, 0:HALF])
    upper = dot(inner, gram[0:HALF, HALF:], 1, 0)
    out[0] = inner
    out[1] = gram[HALF:, HALF:] - dot(upper, upper, 0, 0)
    out[2] = -dot(upper, inner, 0, 0)


def second_half_kernel(half, out):
    inner = inverse_factor(half[1])
    out[0:HALF, 0:HALF] = half[0]
    out[0:HALF, HALF:] = jnp.zeros((HALF, HALF), f32)
    out[HALF:, 0:HALF] = dot(inner, half[2], 1, 0)
    out[HALF:, HALF:] = inner


def squares_kernel(own, column_mine, inverse, factor_mine, squares):
    factor_mine[...] = dot(column_mine[...], inverse[...], 1, 1)
    total = jnp.zeros((1, RANK), f32)
    for x in range(NX):
        c = dot(own[x].reshape(NZ * SHARD, RANK), inverse[...], 1, 1)
        total = total + jnp.sum(c * c, axis=0, keepdims=True)
    for i in range(NY * NC):
        squares[i] = total


def ortho_kernel(power, inverse, row_factor, weights):
    o = dot(power[...], inverse[...], 1, 1)
    row_factor[...] = o * math.sqrt(ROWS)
    weights[...] = 0.05 * dot(o, inverse[...], 1, 0)


def new_right_kernel(pieces, factor_mine, after, out):
    squares = jnp.sum(pieces[...], axis=0)
    out[...] = factor_mine[...] / jnp.sqrt(squares / COLS + 1e-06)


def split(value):
    high = value.astype(bf16)
    return high, (value - high.astype(f32)).astype(bf16)


def momentum_kernel(
    where, own, other, weights, mom, grad, out, token, mom_here, grad_here, full, sems, done
):
    copies = gathered_copies(where, own, other, mom, grad, mom_here, grad_here, full, sems)
    high, low = split(weights[...])
    token[...] = jnp.zeros_like(token)
    for j in range(NX):
        for copy in copies[j]:
            copy.wait()
        fh, fl = split(full[j].reshape(CHUNK, RANK))
        change = dot(fh, high, 1, 1, None) + (dot(fh, low, 1, 1, None) + dot(fl, high, 1, 1, None))
        mom_here[:, columns(j)] = buffer_chunk(mom_here, grad_here, j) - change.T
        copies[j] = pltpu.make_async_copy(
            mom_here.at[:, columns(j)], out.at[:, columns(j)], done.at[j]
        )
        copies[j].start()
    for j in range(NX):
        copies[j].wait()


def spread(value, axis, size):
    copies = jnp.broadcast_to(value[None], (size,) + value.shape)
    return swap(copies, axis)


def swap(pieces, axis):
    return lax.all_to_all(pieces, axis, 0, 0)


def other_core(value):
    return lax.ppermute(value, "c", [(0, 1), (1, 0)])


def sum_along(value, axis, size):
    bit = 1
    while bit < size:
        value = value + lax.ppermute(value, axis, [(i, i ^ bit) for i in range(size)])
        bit *= 2
    return value


def shards(momentum, gradient, right_factor):
    where = jnp.stack([lax.axis_index(a) for a in ("x", "c", "y")]).astype(jnp.int32)
    momentum = pltpu.with_memory_space_constraint(momentum, pltpu.HBM)
    gradient = pltpu.with_memory_space_constraint(gradient, pltpu.HBM)

    halves = [shape(MY_ROWS, PER_CORE)] * 2 + [shape(PER_CORE, MY_ROWS)] * 2
    by_core = call(
        layout_kernel, halves, [SMEM, VMEM, VMEM], (), None, 1_000_000_000, 9_000_000, 24
    )(where, momentum, gradient)
    gathered = spread(right_factor, "z", NZ)
    gathered, *by_core = lax.optimization_barrier((gathered, *by_core))
    buffer_own, buffer_other, own_t, other_t = by_core
    own = spread(gathered, "x", NX)
    own_power = call(
        own_power_kernel, shape(MY_ROWS, RANK), [VMEM, VMEM], (), None, 6 * MACS, 3_000_000
    )(buffer_own, own)
    partial_power = call(
        power_kernel, shape(MY_ROWS, RANK), [HBM, HBM, VMEM],
        [
            pltpu.VMEM((MY_ROWS, PER_CORE), f32),
            pltpu.VMEM((NX, NZ, SHARD, RANK), f32),
            pltpu.SemaphoreType.DMA((PER_CORE // CHUNK, 2)),
        ],
        None, 6 * MACS, 3_000_000,
    )(buffer_other, other_core(own), own_power)

    pieces = swap(partial_power.reshape(NY, MY_ROWS // NY, RANK), "y")
    copies = call(sum_spread_kernel, shape(NY, MY_ROWS // NY, RANK), [VMEM])(pieces)
    power = swap(copies, "y").reshape(MY_ROWS, RANK)

    full = shape(NX, NZ, SHARD, RANK)
    send, some = call(
        send_kernel, [full, shape(SOME, RANK)], [SMEM, VMEM, VMEM],
        [pltpu.VMEM((RANK, RANK), f32)], None, 6 * MACS, 3_000_000,
    )(where, power, other_t)
    arrived = other_core(send)
    keep = call(keep_kernel, full, [VMEM, VMEM, ANY], (), None, 6 * MACS, 3_000_000)(
        power, own_t, some
    )
    sums = keep + arrived
    some = some + other_core(some)
    sums, some = lax.optimization_barrier((sums, some))
    by_x = swap(sums, "x")
    some = sum_along(some, "z", NZ)
    by_x, some = lax.optimization_barrier((by_x, some))
    by_z = call(sum_x_kernel, shape(NZ, SHARD, RANK), [VMEM], nbytes=3_000_000)(by_x)
    by_z, some = lax.optimization_barrier((by_z, some))
    swapped = swap(by_z, "z")
    some = sum_along(some, "x", NX)
    column_mine, copies, gram = call(
        sum_z_kernel,
        [shape(SHARD, RANK), shape(NZ, SHARD, RANK), shape(NY, SOME, RANK)],
        [VMEM, VMEM],
    )(swapped, some)

    gram = swap(gram, "y").reshape(RANK, RANK)
    gram, copies = lax.optimization_barrier((gram, copies))
    half = call(first_half_kernel, shape(3, HALF, HALF), [VMEM], flops=10_000_000_000)(gram)
    gathered = swap(copies, "z")
    copies = call(
        copies_kernel, shape(NX, NZ, SHARD, RANK), [VMEM, ANY], nbytes=3_000_000
    )(gathered, half)
    half, copies = lax.optimization_barrier((half, copies))
    own = swap(copies, "x")
    inverse = call(second_half_kernel, shape(RANK, RANK), [VMEM], flops=10_000_000_000)(half)
    row_factor, weights = call(
        ortho_kernel, [shape(MY_ROWS, RANK)] * 2, [VMEM, VMEM]
    )(power, inverse)
    own, weights, inverse = lax.optimization_barrier((own, weights, inverse))
    factor_mine, squares = call(
        squares_kernel, [shape(SHARD, RANK), shape(NY * NC, 1, RANK)], [VMEM] * 3, (), None,
        6 * MACS, 2_000_000,
    )(own, column_mine, inverse)
    squares = swap(squares, ("y", "c"))
    new_momentum, token = call(
        momentum_kernel, [in_hbm(MY_ROWS, MY_COLS), TOKEN], [SMEM, HBM, HBM, VMEM, HBM, HBM],
        BUFFER_SCRATCH + FULL + SEMS + [pltpu.SemaphoreType.DMA((NX,))],
        [HBM, VMEM], 6 * MACS, 9_000_000,
    )(where, own, other_core(own), weights, momentum, gradient)
    new_right = call(new_right_kernel, shape(SHARD, RANK), [VMEM, VMEM, ANY])(
        squares, factor_mine, token
    )
    return (new_momentum, new_right, row_factor)


def solution(mesh):
    devices = np.asarray(mesh.devices).reshape(NX, NZ, NC, NY)
    grid = Mesh(devices, ("x", "z", "c", "y"))
    fsdp = ("x", "z", "c")
    return jax.shard_map(
        shards,
        mesh=grid,
        in_specs=(P(fsdp, "y"), P(fsdp, "y"), P(("y",) + fsdp, None)),
        out_specs=(P(fsdp, "y"), P(("y",) + fsdp, None), P(fsdp, None)),
        check_vma=False,
    )
```

```python
import math

import jax
import jax.numpy as jnp
import numpy as np
from jax import lax
from jax.experimental import pallas as pl
from jax.experimental.pallas import tpu as pltpu
from jax.sharding import Mesh, PartitionSpec as P

ROWS = 8192
COLS = 28672
RANK = 256
NX, NZ, NC, NY = 4, 8, 2, 8
MY_ROWS = 128
MY_COLS = 3584
SHARD = 56
CHUNK = NZ * NC * SHARD
HALF = 128
GROUP = 8
SOME = RANK // NZ
ORDER = (0, 4, 2, 6, 1, 5, 3, 7)
PER_CORE = MY_COLS // NC
MACS = MY_ROWS * MY_COLS * RANK

highest = lax.Precision.HIGHEST
f32 = jnp.float32
bf16 = jnp.bfloat16
VMEM = pl.BlockSpec(memory_space=pltpu.VMEM)
SMEM = pl.BlockSpec(memory_space=pltpu.SMEM)
ANY = pl.BlockSpec(memory_space=pl.ANY)
HBM = pl.BlockSpec(memory_space=pltpu.HBM)


def dot(a, b, ca, cb, precision=highest):
    return lax.dot_general(
        a, b, (((ca,), (cb,)), ((), ())), precision=precision, preferred_element_type=f32
    )


def shape(*dims):
    return jax.ShapeDtypeStruct(dims, f32)


def in_hbm(*dims):
    return pltpu.HBM(dims, f32)


TOKEN = shape(8, 128)


def call(kernel, out_shape, in_specs, scratch=(), out_specs=None, flops=1_000_000, nbytes=100_000, limit=12):
    return pl.pallas_call(
        kernel,
        out_shape=out_shape,
        in_specs=in_specs,
        out_specs=out_specs or jax.tree.map(lambda _: VMEM, out_shape),
        scratch_shapes=scratch,
        compiler_params=pltpu.CompilerParams(vmem_limit_bytes=limit * 2**20),
        cost_estimate=pl.CostEstimate(
            flops=flops, bytes_accessed=nbytes, transcendentals=0
        ),
    )


def columns(j):
    return pl.ds(j * CHUNK, CHUNK)


def buffer_copies(mom, grad, mom_here, grad_here, sems, j):
    cols = columns(j)
    return [
        pltpu.make_async_copy(mom.at[:, cols], mom_here.at[:, cols], sems.at[j, 0]),
        pltpu.make_async_copy(grad.at[:, cols], grad_here.at[:, cols], sems.at[j, 1]),
    ]


def gathered_copies(where, own, other, mom, grad, mom_here, grad_here, full, sems):
    core = where[1]
    copies = []
    for j in range(NX):
        copies.append(
            [
                pltpu.make_async_copy(own.at[j], full.at[j, :, core], sems.at[j, 2]),
                pltpu.make_async_copy(other.at[j], full.at[j, :, 1 - core], sems.at[j, 3]),
            ]
            + buffer_copies(mom, grad, mom_here, grad_here, sems, j)
        )
        for copy in copies[j]:
            copy.start()
    return copies


def buffer_chunk(mom, grad, j):
    return mom[:, columns(j)] + grad[:, columns(j)].astype(f32)


BUFFER_SCRATCH = [pltpu.VMEM((MY_ROWS, MY_COLS), f32), pltpu.VMEM((MY_ROWS, MY_COLS), bf16)]
SEMS = [pltpu.SemaphoreType.DMA((NX, 4))]
FULL = [pltpu.VMEM((NX, NZ, NC, SHARD, RANK), f32)]


def layout_kernel(where, mom, grad, own, other, own_t, other_t):
    first = where[1] == 0
    for j in range(NX):
        part = buffer_chunk(mom, grad, j).T.reshape(NZ, NC, SHARD, MY_ROWS)
        rows = pl.ds(j * NZ * SHARD, NZ * SHARD)
        own_t[rows] = jnp.where(first, part[:, 0], part[:, 1]).reshape(NZ * SHARD, MY_ROWS)
        other_t[rows] = jnp.where(first, part[:, 1], part[:, 0]).reshape(NZ * SHARD, MY_ROWS)
    for j in range(PER_CORE // CHUNK):
        own[:, columns(j)] = own_t[columns(j)].T
        other[:, columns(j)] = other_t[columns(j)].T


def own_power_kernel(buffer, factor, out):
    total = None
    for j in range(PER_CORE // CHUNK):
        part = factor[j * 2 : j * 2 + 2].reshape(CHUNK, RANK)
        part = dot(buffer[:, columns(j)], part, 1, 0)
        total = part if total is None else total + part
    out[...] = total


def power_kernel(buffer, factor, before, out, here, full, sems):
    copies = []
    for j in range(PER_CORE // CHUNK):
        pair = pl.ds(j * 2, 2)
        copies.append(
            [
                pltpu.make_async_copy(factor.at[pair], full.at[pair], sems.at[j, 0]),
                pltpu.make_async_copy(
                    buffer.at[:, columns(j)], here.at[:, columns(j)], sems.at[j, 1]
                ),
            ]
        )
        for copy in copies[j]:
            copy.start()
    total = before[...]
    for j in range(PER_CORE // CHUNK):
        for copy in copies[j]:
            copy.wait()
        part = full[j * 2 : j * 2 + 2].reshape(CHUNK, RANK)
        total = total + dot(here[:, columns(j)], part, 1, 0)
    out[...] = total


def sum_spread_kernel(pieces, out):
    total = jnp.sum(pieces[...], axis=0)
    for i in range(out.shape[0]):
        out[i] = total


def column_product(power, buffer_t, out):
    for x in range(NX):
        part = dot(buffer_t[pl.ds(x * NZ * SHARD, NZ * SHARD)], power[...], 1, 0)
        out[x] = part.reshape(NZ, SHARD, RANK)


def send_kernel(power, buffer_t, out, gram):
    gram[...] = dot(power[...], power[...], 0, 0)
    column_product(power, buffer_t, out)


def keep_kernel(power, buffer_t, after, out):
    column_product(power, buffer_t, out)


def sum_x_kernel(pieces, out):
    out[...] = (pieces[0] + pieces[1]) + (pieces[2] + pieces[3])


def sum_z_kernel(pieces, gram, mine, copies):
    column = jnp.sum(pieces[...], axis=0)
    mine[...] = column
    for i in range(NZ):
        copies[i, 0:SHARD] = column
        copies[i, SHARD:] = gram[...]


def copies_kernel(pieces, out, gram):
    for i in range(NX):
        out[i] = pieces[:, 0:SHARD]
    for i, z in enumerate(ORDER):
        gram[i * SOME : (i + 1) * SOME] = pieces[z, SHARD:]


def inverse_factor(d):
    row = lax.broadcasted_iota(jnp.int32, (GROUP, HALF), 0)
    col = lax.broadcasted_iota(jnp.int32, (GROUP, HALF), 1)
    groups = [d[g * GROUP : (g + 1) * GROUP] for g in range(HALF // GROUP)]
    for j in range(0, HALF - 2, 2):
        g0, i = divmod(j, GROUP)
        column0 = [None] * len(groups)
        column1 = [None] * len(groups)
        for g in range(g0, len(groups)):
            column0[g] = jnp.broadcast_to(groups[g][:, j : j + 1], (GROUP, HALF))
            column1[g] = jnp.broadcast_to(groups[g][:, j + 1 : j + 2], (GROUP, HALF))
        p = column0[g0][i : i + 1]
        b = column0[g0][i + 1 : i + 2]
        q = column1[g0][i + 1 : i + 2]
        over_p = 1.0 / p
        ratio = b * over_p
        over_q = 1.0 / (q - ratio * b)
        first, second = col[0:1] == j, col[0:1] == j + 1
        line0 = jnp.where(first, 1.0, jnp.where(second, 0.0, groups[g0][i : i + 1]))
        line1 = jnp.where(first, 0.0, jnp.where(second, 1.0, groups[g0][i + 1 : i + 2]))
        line1 = over_q * (line1 - ratio * line0)
        line0 = over_p * line0 - ratio * line1
        line0 = jnp.broadcast_to(line0, (GROUP, HALF))
        line1 = jnp.broadcast_to(line1, (GROUP, HALF))
        pivots = (col == j) | (col == j + 1)
        for g in range(g0, len(groups)):
            rest = jnp.where(pivots, 0.0, groups[g])
            rest = rest - column0[g] * line0 - column1[g] * line1
            groups[g] = jnp.where(row > i + 1, rest, groups[g]) if g == g0 else rest
    odd = row % 2 == 1
    for g in range(len(groups)):
        at = row + g * GROUP
        d = groups[g]
        diagonal = jnp.sum(jnp.where(col == at, d, 0.0), axis=1, keepdims=True)
        diagonal = jnp.broadcast_to(diagonal, (GROUP, HALF))
        below = jnp.sum(jnp.where(col == at - 1, d, 0.0), axis=1, keepdims=True)
        below = jnp.broadcast_to(below, (GROUP, HALF))
        ratio = jnp.where(odd, below / pltpu.roll(diagonal, 1, 0), 0.0)
        scale = lax.rsqrt(diagonal - ratio * below)
        unit = jnp.where(col == at, 1.0, jnp.where(col < at - at % 2, d, 0.0))
        groups[g] = scale * (unit - ratio * pltpu.roll(unit, 1, 0))
    return jnp.concatenate(groups, axis=0)


def first_half_kernel(gram, out):
    inner = inverse_factor(gram[0:HALF, 0:HALF])
    upper = dot(inner, gram[0:HALF, HALF:], 1, 0)
    out[0] = inner
    out[1] = gram[HALF:, HALF:] - dot(upper, upper, 0, 0)
    out[2] = -dot(upper, inner, 0, 0)


def second_half_kernel(half, out):
    inner = inverse_factor(half[1])
    out[0:HALF, 0:HALF] = half[0]
    out[0:HALF, HALF:] = jnp.zeros((HALF, HALF), f32)
    out[HALF:, 0:HALF] = dot(inner, half[2], 1, 0)
    out[HALF:, HALF:] = inner


def squares_kernel(own, column_mine, inverse, factor_mine, squares):
    factor_mine[...] = dot(column_mine[...], inverse[...], 1, 1)
    total = jnp.zeros((1, RANK), f32)
    for x in range(NX):
        c = dot(own[x].reshape(NZ * SHARD, RANK), inverse[...], 1, 1)
        total = total + jnp.sum(c * c, axis=0, keepdims=True)
    for i in range(NY * NC):
        squares[i] = total


def ortho_kernel(power, inverse, row_factor, weights):
    o = dot(power[...], inverse[...], 1, 1)
    row_factor[...] = o * math.sqrt(ROWS)
    weights[...] = 0.05 * dot(o, inverse[...], 1, 0)


def new_right_kernel(pieces, factor_mine, after, out):
    squares = jnp.sum(pieces[...], axis=0)
    out[...] = factor_mine[...] / jnp.sqrt(squares / COLS + 1e-06)


def split(value):
    high = value.astype(bf16)
    return high, (value - high.astype(f32)).astype(bf16)


def momentum_kernel(
    where, own, other, weights, mom, grad, out, token, mom_here, grad_here, full, sems, done
):
    copies = gathered_copies(where, own, other, mom, grad, mom_here, grad_here, full, sems)
    high, low = split(weights[...])
    both = jnp.concatenate([high, low], axis=0)
    token[...] = jnp.zeros_like(token)
    for j in range(NX):
        for copy in copies[j]:
            copy.wait()
        fh, fl = split(full[j].reshape(CHUNK, RANK))
        change = dot(both, fh, 1, 1, None)
        change = change[0:MY_ROWS] + (change[MY_ROWS:] + dot(high, fl, 1, 1, None))
        mom_here[:, columns(j)] = buffer_chunk(mom_here, grad_here, j) - change
        copies[j] = pltpu.make_async_copy(
            mom_here.at[:, columns(j)], out.at[:, columns(j)], done.at[j]
        )
        copies[j].start()
    for j in range(NX):
        copies[j].wait()


def spread(value, axis, size):
    copies = jnp.broadcast_to(value[None], (size,) + value.shape)
    return swap(copies, axis)


def swap(pieces, axis):
    return lax.all_to_all(pieces, axis, 0, 0)


def other_core(value):
    return lax.ppermute(value, "c", [(0, 1), (1, 0)])


def sum_along(value, axis, size):
    bit = 1
    while bit < size:
        value = value + lax.ppermute(value, axis, [(i, i ^ bit) for i in range(size)])
        bit *= 2
    return value


def halve_along_z(value):
    z = lax.axis_index("z")
    for bit in (1, 2, 4):
        size = value.shape[0] // 2
        side = (z // bit) % 2
        mine = lax.dynamic_slice_in_dim(value, side * size, size)
        theirs = lax.dynamic_slice_in_dim(value, (1 - side) * size, size)
        value = mine + lax.ppermute(theirs, "z", [(i, i ^ bit) for i in range(NZ)])
    return value


def shards(momentum, gradient, right_factor):
    where = jnp.stack([lax.axis_index(a) for a in ("x", "c", "y")]).astype(jnp.int32)
    momentum = pltpu.with_memory_space_constraint(momentum, pltpu.HBM)
    gradient = pltpu.with_memory_space_constraint(gradient, pltpu.HBM)

    halves = [shape(MY_ROWS, PER_CORE)] * 2 + [shape(PER_CORE, MY_ROWS)] * 2
    by_core = call(
        layout_kernel, halves, [SMEM, VMEM, VMEM], (), None, 1_000_000_000, 9_000_000, 24
    )(where, momentum, gradient)
    gathered = spread(right_factor, "z", NZ)
    gathered, *by_core = lax.optimization_barrier((gathered, *by_core))
    buffer_own, buffer_other, own_t, other_t = by_core
    own = spread(gathered, "x", NX)
    own_power = call(
        own_power_kernel, shape(MY_ROWS, RANK), [VMEM, VMEM], (), None, 6 * MACS, 3_000_000
    )(buffer_own, own)
    partial_power = call(
        power_kernel, shape(MY_ROWS, RANK), [HBM, HBM, VMEM],
        [
            pltpu.VMEM((MY_ROWS, PER_CORE), f32),
            pltpu.VMEM((NX, NZ, SHARD, RANK), f32),
            pltpu.SemaphoreType.DMA((PER_CORE // CHUNK, 2)),
        ],
        None, 6 * MACS, 3_000_000,
    )(buffer_other, other_core(own), own_power)

    pieces = swap(partial_power.reshape(NY, MY_ROWS // NY, RANK), "y")
    copies = call(sum_spread_kernel, shape(NY, MY_ROWS // NY, RANK), [VMEM])(pieces)
    power = swap(copies, "y").reshape(MY_ROWS, RANK)

    full = shape(NX, NZ, SHARD, RANK)
    send, gram = call(
        send_kernel, [full, shape(RANK, RANK)], [VMEM, VMEM], (), None, 6 * MACS, 3_000_000
    )(power, other_t)
    arrived = other_core(send)
    keep = call(keep_kernel, full, [VMEM, VMEM, ANY], (), None, 6 * MACS, 3_000_000)(
        power, own_t, gram
    )
    sums = keep + arrived
    gram = gram + other_core(gram)
    sums, gram = lax.optimization_barrier((sums, gram))
    by_x = swap(sums, "x")
    gram = halve_along_z(gram)
    by_x, gram = lax.optimization_barrier((by_x, gram))
    by_z = call(sum_x_kernel, shape(NZ, SHARD, RANK), [VMEM], nbytes=3_000_000)(by_x)
    by_z, gram = lax.optimization_barrier((by_z, gram))
    swapped = swap(by_z, "z")
    gram = sum_along(gram, "x", NX)
    column_mine, copies = call(
        sum_z_kernel, [shape(SHARD, RANK), shape(NZ, SHARD + SOME, RANK)], [VMEM, VMEM]
    )(swapped, gram)

    copies, gram = call(
        copies_kernel, [in_hbm(NX, NZ, SHARD, RANK), shape(RANK, RANK)], [VMEM], nbytes=3_000_000
    )(swap(copies, "z"))
    half = call(first_half_kernel, shape(3, HALF, HALF), [VMEM], flops=10_000_000_000)(gram)
    own = swap(copies, "x")
    inverse = call(second_half_kernel, shape(RANK, RANK), [VMEM], flops=10_000_000_000)(half)
    row_factor, weights = call(
        ortho_kernel, [shape(MY_ROWS, RANK)] * 2, [VMEM, VMEM]
    )(power, inverse)
    own, weights, inverse = lax.optimization_barrier((own, weights, inverse))
    factor_mine, squares = call(
        squares_kernel, [shape(SHARD, RANK), shape(NY * NC, 1, RANK)], [VMEM] * 3, (), None,
        6 * MACS, 2_000_000,
    )(own, column_mine, inverse)
    squares = swap(squares, ("y", "c"))
    new_momentum, token = call(
        momentum_kernel, [in_hbm(MY_ROWS, MY_COLS), TOKEN], [SMEM, HBM, HBM, VMEM, HBM, HBM],
        BUFFER_SCRATCH + FULL + SEMS + [pltpu.SemaphoreType.DMA((NX,))],
        [HBM, VMEM], 6 * MACS, 9_000_000,
    )(where, own, other_core(own), weights, momentum, gradient)
    new_right = call(new_right_kernel, shape(SHARD, RANK), [VMEM, VMEM, ANY])(
        squares, factor_mine, token
    )
    return (new_momentum, new_right, row_factor)


def solution(mesh):
    devices = np.asarray(mesh.devices).reshape(NX, NZ, NC, NY)
    grid = Mesh(devices, ("x", "z", "c", "y"))
    fsdp = ("x", "z", "c")
    return jax.shard_map(
        shards,
        mesh=grid,
        in_specs=(P(fsdp, "y"), P(fsdp, "y"), P(("y",) + fsdp, None)),
        out_specs=(P(fsdp, "y"), P(("y",) + fsdp, None), P(fsdp, None)),
        check_vma=False,
    )
```

```python
import math

import jax
import jax.numpy as jnp
import numpy as np
from jax import lax
from jax.experimental import pallas as pl
from jax.experimental.pallas import tpu as pltpu
from jax.sharding import Mesh, PartitionSpec as P

ROWS = 8192
COLS = 28672
RANK = 256
NX, NZ, NC, NY = 4, 8, 2, 8
MY_ROWS = 128
MY_COLS = 3584
SHARD = 56
CHUNK = NZ * NC * SHARD
HALF = 128
GROUP = 8
SOME = RANK // NZ
ORDER = (0, 4, 2, 6, 1, 5, 3, 7)
PER_CORE = MY_COLS // NC
MACS = MY_ROWS * MY_COLS * RANK

highest = lax.Precision.HIGHEST
f32 = jnp.float32
bf16 = jnp.bfloat16
VMEM = pl.BlockSpec(memory_space=pltpu.VMEM)
SMEM = pl.BlockSpec(memory_space=pltpu.SMEM)
ANY = pl.BlockSpec(memory_space=pl.ANY)
HBM = pl.BlockSpec(memory_space=pltpu.HBM)


def dot(a, b, ca, cb, precision=highest):
    return lax.dot_general(
        a, b, (((ca,), (cb,)), ((), ())), precision=precision, preferred_element_type=f32
    )


def shape(*dims):
    return jax.ShapeDtypeStruct(dims, f32)


def in_hbm(*dims):
    return pltpu.HBM(dims, f32)


TOKEN = shape(8, 128)


def call(kernel, out_shape, in_specs, scratch=(), out_specs=None, flops=1_000_000, nbytes=100_000, limit=12):
    return pl.pallas_call(
        kernel,
        out_shape=out_shape,
        in_specs=in_specs,
        out_specs=out_specs or jax.tree.map(lambda _: VMEM, out_shape),
        scratch_shapes=scratch,
        compiler_params=pltpu.CompilerParams(vmem_limit_bytes=limit * 2**20),
        cost_estimate=pl.CostEstimate(
            flops=flops, bytes_accessed=nbytes, transcendentals=0
        ),
    )


def columns(j):
    return pl.ds(j * CHUNK, CHUNK)


def buffer_copies(mom, grad, mom_here, grad_here, sems, j):
    cols = columns(j)
    return [
        pltpu.make_async_copy(mom.at[:, cols], mom_here.at[:, cols], sems.at[j, 0]),
        pltpu.make_async_copy(grad.at[:, cols], grad_here.at[:, cols], sems.at[j, 1]),
    ]


def gathered_copies(where, own, other, mom, grad, mom_here, grad_here, full, sems):
    core = where[1]
    copies = []
    for j in range(NX):
        copies.append(
            [
                pltpu.make_async_copy(own.at[j], full.at[j, :, core], sems.at[j, 2]),
                pltpu.make_async_copy(other.at[j], full.at[j, :, 1 - core], sems.at[j, 3]),
            ]
            + buffer_copies(mom, grad, mom_here, grad_here, sems, j)
        )
        for copy in copies[j]:
            copy.start()
    return copies


def buffer_chunk(mom, grad, j):
    return mom[:, columns(j)] + grad[:, columns(j)].astype(f32)


BUFFER_SCRATCH = [pltpu.VMEM((MY_ROWS, MY_COLS), f32), pltpu.VMEM((MY_ROWS, MY_COLS), bf16)]
SEMS = [pltpu.SemaphoreType.DMA((NX, 4))]
FULL = [pltpu.VMEM((NX, NZ, NC, SHARD, RANK), f32)]


def layout_kernel(where, mom, grad, own, other, own_t, other_t):
    first = where[1] == 0
    for j in range(NX):
        part = buffer_chunk(mom, grad, j).T.reshape(NZ, NC, SHARD, MY_ROWS)
        rows = pl.ds(j * NZ * SHARD, NZ * SHARD)
        own_t[rows] = jnp.where(first, part[:, 0], part[:, 1]).reshape(NZ * SHARD, MY_ROWS)
        other_t[rows] = jnp.where(first, part[:, 1], part[:, 0]).reshape(NZ * SHARD, MY_ROWS)
    for j in range(PER_CORE // CHUNK):
        own[:, columns(j)] = own_t[columns(j)].T
        other[:, columns(j)] = other_t[columns(j)].T


def own_power_kernel(buffer, factor, out):
    total = None
    for j in range(PER_CORE // CHUNK):
        part = factor[j * 2 : j * 2 + 2].reshape(CHUNK, RANK)
        part = dot(buffer[:, columns(j)], part, 1, 0)
        total = part if total is None else total + part
    out[...] = total


def power_kernel(buffer, factor, before, out, here, full, sems):
    copies = []
    for j in range(PER_CORE // CHUNK):
        pair = pl.ds(j * 2, 2)
        copies.append(
            [
                pltpu.make_async_copy(factor.at[pair], full.at[pair], sems.at[j, 0]),
                pltpu.make_async_copy(
                    buffer.at[:, columns(j)], here.at[:, columns(j)], sems.at[j, 1]
                ),
            ]
        )
        for copy in copies[j]:
            copy.start()
    total = before[...]
    for j in range(PER_CORE // CHUNK):
        for copy in copies[j]:
            copy.wait()
        part = full[j * 2 : j * 2 + 2].reshape(CHUNK, RANK)
        total = total + dot(here[:, columns(j)], part, 1, 0)
    out[...] = total


def sum_spread_kernel(pieces, out):
    total = jnp.sum(pieces[...], axis=0)
    for i in range(out.shape[0]):
        out[i] = total


def column_product(power, buffer_t, out):
    for x in range(NX):
        part = dot(buffer_t[pl.ds(x * NZ * SHARD, NZ * SHARD)], power[...], 1, 0)
        out[x] = part.reshape(NZ, SHARD, RANK)


def send_kernel(power, buffer_t, out, gram):
    gram[...] = dot(power[...], power[...], 0, 0)
    column_product(power, buffer_t, out)


def keep_kernel(power, buffer_t, arrived, out):
    for x in range(NX):
        part = dot(buffer_t[pl.ds(x * NZ * SHARD, NZ * SHARD)], power[...], 1, 0)
        out[x] = part.reshape(NZ, SHARD, RANK) + arrived[x]


def sum_x_kernel(pieces, out):
    out[...] = (pieces[0] + pieces[1]) + (pieces[2] + pieces[3])


def sum_z_kernel(pieces, gram, mine, copies):
    column = jnp.sum(pieces[...], axis=0)
    mine[...] = column
    for i in range(NZ):
        copies[i, 0:SHARD] = column
        copies[i, SHARD:] = gram[...]


def copies_kernel(pieces, out, gram, sems):
    copies = [
        pltpu.make_async_copy(pieces.at[:, pl.ds(0, SHARD)], out.at[i], sems.at[i])
        for i in range(NX)
    ]
    for copy in copies:
        copy.start()
    for i, z in enumerate(ORDER):
        gram[i * SOME : (i + 1) * SOME] = pieces[z, SHARD:]
    for copy in copies:
        copy.wait()


def inverse_factor(d):
    row = lax.broadcasted_iota(jnp.int32, (GROUP, HALF), 0)
    col = lax.broadcasted_iota(jnp.int32, (GROUP, HALF), 1)
    groups = [d[g * GROUP : (g + 1) * GROUP] for g in range(HALF // GROUP)]
    for j in range(0, HALF - 2, 2):
        g0, i = divmod(j, GROUP)
        column0 = [None] * len(groups)
        column1 = [None] * len(groups)
        for g in range(g0, len(groups)):
            column0[g] = jnp.broadcast_to(groups[g][:, j : j + 1], (GROUP, HALF))
            column1[g] = jnp.broadcast_to(groups[g][:, j + 1 : j + 2], (GROUP, HALF))
        p = column0[g0][i : i + 1]
        b = column0[g0][i + 1 : i + 2]
        q = column1[g0][i + 1 : i + 2]
        over_p = 1.0 / p
        ratio = b * over_p
        over_q = 1.0 / (q - ratio * b)
        first, second = col[0:1] == j, col[0:1] == j + 1
        line0 = jnp.where(first, 1.0, jnp.where(second, 0.0, groups[g0][i : i + 1]))
        line1 = jnp.where(first, 0.0, jnp.where(second, 1.0, groups[g0][i + 1 : i + 2]))
        line1 = over_q * (line1 - ratio * line0)
        line0 = over_p * line0 - ratio * line1
        line0 = jnp.broadcast_to(line0, (GROUP, HALF))
        line1 = jnp.broadcast_to(line1, (GROUP, HALF))
        pivots = (col == j) | (col == j + 1)
        for g in range(g0, len(groups)):
            rest = jnp.where(pivots, 0.0, groups[g])
            rest = rest - column0[g] * line0 - column1[g] * line1
            groups[g] = jnp.where(row > i + 1, rest, groups[g]) if g == g0 else rest
    odd = row % 2 == 1
    for g in range(len(groups)):
        at = row + g * GROUP
        d = groups[g]
        diagonal = jnp.sum(jnp.where(col == at, d, 0.0), axis=1, keepdims=True)
        diagonal = jnp.broadcast_to(diagonal, (GROUP, HALF))
        below = jnp.sum(jnp.where(col == at - 1, d, 0.0), axis=1, keepdims=True)
        below = jnp.broadcast_to(below, (GROUP, HALF))
        ratio = jnp.where(odd, below / pltpu.roll(diagonal, 1, 0), 0.0)
        scale = lax.rsqrt(diagonal - ratio * below)
        unit = jnp.where(col == at, 1.0, jnp.where(col < at - at % 2, d, 0.0))
        groups[g] = scale * (unit - ratio * pltpu.roll(unit, 1, 0))
    return jnp.concatenate(groups, axis=0)


def first_half_kernel(gram, out):
    inner = inverse_factor(gram[0:HALF, 0:HALF])
    upper = dot(inner, gram[0:HALF, HALF:], 1, 0)
    out[0] = inner
    out[1] = gram[HALF:, HALF:] - dot(upper, upper, 0, 0)
    out[2] = -dot(upper, inner, 0, 0)


def second_half_kernel(half, out):
    inner = inverse_factor(half[1])
    out[0:HALF, 0:HALF] = half[0]
    out[0:HALF, HALF:] = jnp.zeros((HALF, HALF), f32)
    out[HALF:, 0:HALF] = dot(inner, half[2], 1, 0)
    out[HALF:, HALF:] = inner


def squares_kernel(own, column_mine, inverse, factor_mine, squares):
    factor_mine[...] = dot(column_mine[...], inverse[...], 1, 1)
    total = jnp.zeros((1, RANK), f32)
    for x in range(NX):
        c = dot(own[x].reshape(NZ * SHARD, RANK), inverse[...], 1, 1)
        total = total + jnp.sum(c * c, axis=0, keepdims=True)
    for i in range(NY * NC):
        squares[i] = total


def ortho_kernel(power, inverse, row_factor, weights):
    o = dot(power[...], inverse[...], 1, 1)
    row_factor[...] = o * math.sqrt(ROWS)
    weights[...] = 0.05 * dot(o, inverse[...], 1, 0)


def new_right_kernel(pieces, factor_mine, after, out):
    squares = jnp.sum(pieces[...], axis=0)
    out[...] = factor_mine[...] / jnp.sqrt(squares / COLS + 1e-06)


def split(value):
    high = value.astype(bf16)
    return high, (value - high.astype(f32)).astype(bf16)


def momentum_kernel(
    where, own, other, weights, mom, grad, out, token, mom_here, grad_here, full, sems, done
):
    copies = gathered_copies(where, own, other, mom, grad, mom_here, grad_here, full, sems)
    high, low = split(weights[...])
    both = jnp.concatenate([high, low], axis=0)
    token[...] = jnp.zeros_like(token)
    for j in range(NX):
        for copy in copies[j]:
            copy.wait()
        fh, fl = split(full[j].reshape(CHUNK, RANK))
        change = dot(both, fh, 1, 1, None)
        change = change[0:MY_ROWS] + (change[MY_ROWS:] + dot(high, fl, 1, 1, None))
        mom_here[:, columns(j)] = buffer_chunk(mom_here, grad_here, j) - change
        copies[j] = pltpu.make_async_copy(
            mom_here.at[:, columns(j)], out.at[:, columns(j)], done.at[j]
        )
        copies[j].start()
    for j in range(NX):
        copies[j].wait()


def spread(value, axis, size):
    copies = jnp.broadcast_to(value[None], (size,) + value.shape)
    return swap(copies, axis)


def swap(pieces, axis):
    return lax.all_to_all(pieces, axis, 0, 0)


def other_core(value):
    return lax.ppermute(value, "c", [(0, 1), (1, 0)])


def sum_along(value, axis, size):
    bit = 1
    while bit < size:
        value = value + lax.ppermute(value, axis, [(i, i ^ bit) for i in range(size)])
        bit *= 2
    return value


def halve_along_z(value):
    z = lax.axis_index("z")
    for bit in (1, 2, 4):
        size = value.shape[0] // 2
        side = (z // bit) % 2
        mine = lax.dynamic_slice_in_dim(value, side * size, size)
        theirs = lax.dynamic_slice_in_dim(value, (1 - side) * size, size)
        value = mine + lax.ppermute(theirs, "z", [(i, i ^ bit) for i in range(NZ)])
    return value


def shards(momentum, gradient, right_factor):
    where = jnp.stack([lax.axis_index(a) for a in ("x", "c", "y")]).astype(jnp.int32)
    momentum = pltpu.with_memory_space_constraint(momentum, pltpu.HBM)
    gradient = pltpu.with_memory_space_constraint(gradient, pltpu.HBM)

    halves = [shape(MY_ROWS, PER_CORE)] * 2 + [shape(PER_CORE, MY_ROWS)] * 2
    by_core = call(
        layout_kernel, halves, [SMEM, VMEM, VMEM], (), None, 1_000_000_000, 9_000_000, 24
    )(where, momentum, gradient)
    gathered = spread(right_factor, "z", NZ)
    gathered, *by_core = lax.optimization_barrier((gathered, *by_core))
    buffer_own, buffer_other, own_t, other_t = by_core
    own = spread(gathered, "x", NX)
    own_power = call(
        own_power_kernel, shape(MY_ROWS, RANK), [VMEM, VMEM], (), None, 6 * MACS, 3_000_000
    )(buffer_own, own)
    partial_power = call(
        power_kernel, shape(MY_ROWS, RANK), [HBM, HBM, VMEM],
        [
            pltpu.VMEM((MY_ROWS, PER_CORE), f32),
            pltpu.VMEM((NX, NZ, SHARD, RANK), f32),
            pltpu.SemaphoreType.DMA((PER_CORE // CHUNK, 2)),
        ],
        None, 6 * MACS, 3_000_000,
    )(buffer_other, other_core(own), own_power)

    pieces = swap(partial_power.reshape(NY, MY_ROWS // NY, RANK), "y")
    copies = call(sum_spread_kernel, shape(NY, MY_ROWS // NY, RANK), [VMEM])(pieces)
    power = swap(copies, "y").reshape(MY_ROWS, RANK)

    full = shape(NX, NZ, SHARD, RANK)
    send, gram = call(
        send_kernel, [full, shape(RANK, RANK)], [VMEM, VMEM], (), None, 6 * MACS, 3_000_000
    )(power, other_t)
    arrived = other_core(send)
    sums = call(
        keep_kernel, in_hbm(NX, NZ, SHARD, RANK), [VMEM] * 3, (), None, 6 * MACS, 5_000_000
    )(power, own_t, arrived)
    gram = gram + other_core(gram)
    sums, gram = lax.optimization_barrier((sums, gram))
    by_x = swap(sums, "x")
    gram = halve_along_z(gram)
    by_x, gram = lax.optimization_barrier((by_x, gram))
    by_z = call(sum_x_kernel, shape(NZ, SHARD, RANK), [VMEM], nbytes=3_000_000)(by_x)
    by_z, gram = lax.optimization_barrier((by_z, gram))
    swapped = swap(by_z, "z")
    gram = sum_along(gram, "x", NX)
    column_mine, copies = call(
        sum_z_kernel, [shape(SHARD, RANK), shape(NZ, SHARD + SOME, RANK)], [VMEM, VMEM]
    )(swapped, gram)

    copies, gram = call(
        copies_kernel, [in_hbm(NX, NZ, SHARD, RANK), shape(RANK, RANK)], [VMEM],
        [pltpu.SemaphoreType.DMA((NX,))], [HBM, VMEM], nbytes=3_000_000,
    )(swap(copies, "z"))
    half = call(first_half_kernel, shape(3, HALF, HALF), [VMEM], flops=10_000_000_000)(gram)
    own = swap(copies, "x")
    inverse = call(second_half_kernel, shape(RANK, RANK), [VMEM], flops=10_000_000_000)(half)
    row_factor, weights = call(
        ortho_kernel, [shape(MY_ROWS, RANK)] * 2, [VMEM, VMEM]
    )(power, inverse)
    own, weights, inverse = lax.optimization_barrier((own, weights, inverse))
    factor_mine, squares = call(
        squares_kernel, [shape(SHARD, RANK), shape(NY * NC, 1, RANK)], [VMEM] * 3, (), None,
        6 * MACS, 2_000_000,
    )(own, column_mine, inverse)
    squares = swap(squares, ("y", "c"))
    new_momentum, token = call(
        momentum_kernel, [in_hbm(MY_ROWS, MY_COLS), TOKEN], [SMEM, HBM, HBM, VMEM, HBM, HBM],
        BUFFER_SCRATCH + FULL + SEMS + [pltpu.SemaphoreType.DMA((NX,))],
        [HBM, VMEM], 6 * MACS, 9_000_000,
    )(where, own, other_core(own), weights, momentum, gradient)
    new_right = call(new_right_kernel, shape(SHARD, RANK), [VMEM, VMEM, ANY])(
        squares, factor_mine, token
    )
    return (new_momentum, new_right, row_factor)


def solution(mesh):
    devices = np.asarray(mesh.devices).reshape(NX, NZ, NC, NY)
    grid = Mesh(devices, ("x", "z", "c", "y"))
    fsdp = ("x", "z", "c")
    return jax.shard_map(
        shards,
        mesh=grid,
        in_specs=(P(fsdp, "y"), P(fsdp, "y"), P(("y",) + fsdp, None)),
        out_specs=(P(fsdp, "y"), P(("y",) + fsdp, None), P(fsdp, None)),
        check_vma=False,
    )
```
